32 devices in a mesh: seq: 16 (over z, y, x), head: 2 (over core).
Axes of the slice: x: 2, y: 2, z: 4, core: 2. Of those that a mesh axis runs over, the one named last changes fastest.
Arguments:
- query_rows: bfloat16 [16384, 1536], P(('seq', 'head')), may hold values from -150 to 150
- key_rows: bfloat16 [16384, 1536], P(('seq', 'head')), may hold values from -4 to 4
- value_rows: bfloat16 [16384, 1536], P(('seq', 'head')), may hold values from -6 to 6
- out_grad: bfloat16 [16384, 1536], P(('seq', 'head')), may hold values from -180 to 180
- key_blocks: int32 [32, 3], replicated, may hold values from 0 to 31, as said below
- block_counts: int32 [32], replicated, may hold values from 1 to 3
Outputs:
- query_grad: bfloat16 [16384, 1536], P(('seq', 'head'))
- key_grad: bfloat16 [16384, 1536], P(('seq', 'head'))
- value_grad: bfloat16 [16384, 1536], P(('seq', 'head'))
The draws below stay inside these ranges and needn't reach their ends.
Inputs may be any that keep to these rules, and one draw needn't show every extreme that they name: `key_blocks`: row b lists 3 different key blocks; its first entry is b itself and the others lie within 2 blocks of b.
All inputs are finite; a program needn't handle non-finite values.
Results may differ from the reference program's by a relative error of at most 0.0051.
Values may be sent and summed in bfloat16 or wider, within the bound.
No kernel may reach another device: no remote copies, remote signals or barrier semaphores. Data moves between devices by JAX's collectives and lax.ppermute only.
A program may use at most 192 MiB of HBM per device.

```python
import jax
import jax.numpy as jnp
from jax import lax

HEADS = 12
HEAD_DIM = 128
BLOCK = 512
RADIUS = 2
MAXK = 3
NBLOCKS = 32
TOKENS = 16384


def shared_rows(key, width):
    base_rows = jnp.clip(jax.random.normal(key, (TOKENS, width), jnp.float32), -4.0, 4.0)
    picked = jax.random.randint(jax.random.fold_in(key, 1), (TOKENS,), 0, 64) == 0
    picked = picked & (jnp.arange(TOKENS) % 2 == 0)
    strength = jnp.exp(jax.random.uniform(jax.random.fold_in(key, 2), (TOKENS,), jnp.float32, jnp.log(150.0), jnp.log(400.0)))
    limit = jnp.where(picked, jnp.minimum(4.0, 150.0 * HEAD_DIM ** 0.5 / strength), 4.0)
    base_rows = jnp.clip(base_rows, -limit[:, None], limit[:, None])
    return base_rows


def draw_key_rows(key, part):
    base_rows = shared_rows(key, HEADS * HEAD_DIM)
    return base_rows.astype(jnp.bfloat16)


def draw_query_rows(key, part):
    key = jax.random.fold_in(key, 5)
    own_rows = jnp.clip(jax.random.normal(key, (TOKENS, HEADS * HEAD_DIM), jnp.float32), -4.0, 4.0)
    return own_rows.astype(jnp.bfloat16)


def draw_key_blocks(key, part):
    key = jax.random.fold_in(key, 7)
    block_ids = jnp.arange(NBLOCKS, dtype=jnp.int32)
    offsets = jnp.concatenate([jnp.arange(-RADIUS, 0), jnp.arange(1, RADIUS + 1)]).astype(jnp.int32)
    targets = block_ids[:, None] + offsets[None, :]
    outside = ((targets < 0) | (targets >= NBLOCKS)).astype(jnp.int32)
    ranks = jax.random.randint(key, (NBLOCKS, 2 * RADIUS), 0, 2 ** 20) * (2 * RADIUS) + jnp.arange(2 * RADIUS, dtype=jnp.int32)[None, :]
    ranks = ranks + outside * 2 ** 28
    ranking = jnp.argsort(ranks, axis=1)
    chosen = jnp.take_along_axis(targets, ranking[:, :MAXK - 1], axis=1)
    return jnp.concatenate([block_ids[:, None], chosen], axis=1).astype(jnp.int32)


def draw_block_counts(key, part):
    key = jax.random.fold_in(key, 9)
    drawn = jax.random.randint(key, (NBLOCKS,), 1, MAXK + 1)
    fullest = jax.random.randint(jax.random.fold_in(key, 1), (), 0, NBLOCKS)
    emptiest = (fullest + 1 + jax.random.randint(jax.random.fold_in(key, 2), (), 0, NBLOCKS - 1)) % NBLOCKS
    drawn = drawn.at[fullest].set(MAXK).at[emptiest].set(1)
    return drawn.astype(jnp.int32)


def block_scale(key, dims, split, smallest, largest):
    def one(axis_at, parts):
        draws = jax.random.uniform(jax.random.fold_in(jax.random.fold_in(key, 6), axis_at), (parts,), jnp.float32, smallest / len(split), largest / len(split))
        return jnp.repeat(jnp.exp(draws), dims[axis_at] // parts).reshape((-1,) + (1,) * (len(dims) - axis_at - 1))

    loudness = one(*split[0])
    for cut in split[1:]:
        loudness = loudness * one(*cut)
    return loudness


def noise(stream_key, shape, scale, bound, cuts=(), kind=jnp.bfloat16):
    result = jax.random.normal(stream_key, shape, jnp.float32) * scale
    if len(cuts) > 0:
        result = block_scale(stream_key, shape, cuts, -0.22, 0.18) * result
    return jnp.clip(result, min=-bound, max=bound).astype(kind)


def setup_inputs(seed: int = 0) -> dict:
    key_list = jax.random.split(jax.random.key(seed), 7)
    query_rows = draw_query_rows(jax.random.fold_in(key_list[6], 71), 0)
    key_rows = draw_key_rows(jax.random.fold_in(key_list[6], 71), 0)
    value_rows = noise(key_list[2], (TOKENS, HEADS * HEAD_DIM), 1.0, 6.0, ((0, 32),))
    out_grad = noise(key_list[3], (TOKENS, HEADS * HEAD_DIM), 30.0, 180.0, ((0, 32),))
    key_blocks = draw_key_blocks(jax.random.fold_in(key_list[6], 71), 0)
    block_counts = draw_block_counts(jax.random.fold_in(key_list[6], 71), 0)
    return dict(query_rows=query_rows, key_rows=key_rows, value_rows=value_rows, out_grad=out_grad, key_blocks=key_blocks, block_counts=block_counts)


def lower_round(values):
    return lax.optimization_barrier(values.astype(jnp.bfloat16)).astype(jnp.float32)


def reference(query_rows, key_rows, value_rows, out_grad, key_blocks, block_counts):
    score_scale = HEAD_DIM ** -0.5
    block_total = TOKENS // BLOCK
    query_heads = query_rows.reshape(TOKENS, HEADS, HEAD_DIM)
    key_heads = key_rows.reshape(TOKENS, HEADS, HEAD_DIM)
    value_heads = value_rows.reshape(TOKENS, HEADS, HEAD_DIM)
    grad_heads = out_grad.reshape(TOKENS, HEADS, HEAD_DIM)
    slot_range = jnp.arange(MAXK, dtype=jnp.int32)

    def per_block(carry, block_index):
        key_acc, value_acc = carry
        row_start = (block_index * BLOCK).astype(jnp.int32)
        query_block = lax.dynamic_slice_in_dim(query_heads, row_start, BLOCK, 0).astype(jnp.float32)
        grad_block = lax.dynamic_slice_in_dim(grad_heads, row_start, BLOCK, 0).astype(jnp.float32)
        listed_blocks = key_blocks[block_index]
        live_slots = slot_range < block_counts[block_index]
        key_starts = [(listed_blocks[slot_index] * BLOCK).astype(jnp.int32) for slot_index in range(MAXK)]
        key_stack = jnp.stack([lax.dynamic_slice_in_dim(key_heads, start_row, BLOCK, 0) for start_row in key_starts]).astype(jnp.float32)
        value_stack = jnp.stack([lax.dynamic_slice_in_dim(value_heads, start_row, BLOCK, 0) for start_row in key_starts]).astype(jnp.float32)
        scores = jnp.einsum("qhd,skhd->shqk", query_block, key_stack) * score_scale
        row_peak = jnp.max(jnp.where(live_slots[:, None, None], jnp.max(scores, axis=3), -jnp.inf), axis=0)
        shifted = jnp.exp(scores - row_peak[None, :, :, None])
        row_total = jnp.sum(jnp.where(live_slots[:, None, None, None], shifted, 0.0), axis=(0, 3))
        log_total = row_peak + jnp.log(row_total)
        live_float = live_slots.astype(scores.dtype)
        weights = jnp.exp(scores - log_total[None, :, :, None]) * live_float[:, None, None, None]
        weight_grads = jnp.einsum("qhd,skhd->shqk", grad_block, value_stack)
        row_delta = jnp.sum(weights * weight_grads, axis=(0, 3))
        score_grads = lower_round(weights * (weight_grads - row_delta[None, :, :, None]))
        weights_low = lower_round(weights)
        query_part = jnp.einsum("shqk,skhd->qhd", score_grads, key_stack) * score_scale
        key_parts = jnp.einsum("shqk,qhd->skhd", score_grads, query_block) * score_scale
        value_parts = jnp.einsum("shqk,qhd->skhd", weights_low, grad_block)
        for slot_index in range(MAXK):
            start_row = key_starts[slot_index]
            key_acc = lax.dynamic_update_slice_in_dim(key_acc, lax.dynamic_slice_in_dim(key_acc, start_row, BLOCK, 0) + key_parts[slot_index], start_row, 0)
            value_acc = lax.dynamic_update_slice_in_dim(value_acc, lax.dynamic_slice_in_dim(value_acc, start_row, BLOCK, 0) + value_parts[slot_index], start_row, 0)
        return (key_acc, value_acc), query_part.astype(jnp.bfloat16)

    empty = jnp.zeros((TOKENS, HEADS, HEAD_DIM), jnp.float32)
    (key_acc, value_acc), query_parts = lax.scan(per_block, (empty, empty), jnp.arange(block_total, dtype=jnp.int32))
    query_grad = query_parts.reshape(TOKENS, HEADS * HEAD_DIM)
    key_grad = key_acc.astype(jnp.bfloat16).reshape(TOKENS, HEADS * HEAD_DIM)
    value_grad = value_acc.astype(jnp.bfloat16).reshape(TOKENS, HEADS * HEAD_DIM)
    return (query_grad, key_grad, value_grad)
```

```python
import functools
import math

import jax
import jax.numpy as jnp
from jax import lax
from jax.experimental import pallas as pl
from jax.experimental.pallas import tpu as pltpu
from jax.sharding import PartitionSpec as P

HEADS = 12
HEAD_DIM = 128
BLOCK = 512
MAXK = 3
CHUNKS = (1, 1, 1, 1, 1, 1)
SCALE = HEAD_DIM ** -0.5
LOG_SCALE = SCALE * math.log2(math.e)
LOWEST = -1e30
VMEM_LIMIT = 40 * 1024 * 1024


def pair_rows(left, right):
    return lax.dot_general(
        left, right, (((1,), (1,)), ((), ())), preferred_element_type=jnp.float32
    )


def product(left, right):
    return jnp.dot(left, right, preferred_element_type=jnp.float32)


def is_live(place, lists, counts, query, key):
    chip, core, chips = place[0], place[1], place[2]
    odd = chip & 1
    origin, slot = query >> 1, query & 1
    step = jnp.where(origin == 1, 1 - 2 * odd, 2 * odd - 1)
    source = chip + jnp.where(origin == 0, 0, step)
    inside = (source >= 0) & (source < chips)
    query_block = 2 * jnp.clip(source, 0, chips - 1) + (core ^ slot)
    key_block = 2 * chip + (core ^ key)
    count = counts[query_block]
    found = lists[query_block * MAXK] == key_block
    for at in range(1, MAXK):
        found = found | ((lists[query_block * MAXK + at] == key_block) & (at < count))
    return found & inside


def for_live_pairs(scalars, first, last, step):
    place, lists, counts = scalars

    def candidate(index, carry):
        query, key = index >> 1, index & 1

        @pl.when(is_live(place, lists, counts, query, key))
        def _():
            step(query, key)

        return carry

    lax.fori_loop(2 * first, 2 * last, candidate, 0)


def fetch(copies, sem):
    started = [
        pltpu.make_async_copy(source, target, sem.at[at])
        for at, (source, target) in enumerate(copies)
    ]
    for copy in started:
        copy.start()
    for copy in started:
        copy.wait()


def key_copies(place, keys, lane, width, key_buf, value_buf):
    key_mine, key_other, value_mine, value_other = keys
    half = key_other.shape[1]
    own_columns = pl.ds(pl.multiple_of(place[1] * half + lane, HEAD_DIM), width)
    far_columns = pl.ds(lane, width)
    return [
        (key_mine.at[:, own_columns], key_buf.at[0]),
        (key_other.at[:, far_columns], key_buf.at[1]),
        (value_mine.at[:, own_columns], value_buf.at[0]),
        (value_other.at[:, far_columns], value_buf.at[1]),
    ]


def stats_step(heads, base, key_buf, value_buf, rows_buf, stats_ref):
    def step(query, key):
        for head in range(heads):
            lanes = slice(head * HEAD_DIM, (head + 1) * HEAD_DIM)
            at = query - base
            scores = pair_rows(key_buf[key, :, lanes], rows_buf[at, 0, :, lanes])
            weight_grads = pair_rows(value_buf[key, :, lanes], rows_buf[at, 1, :, lanes])
            peak_here = jnp.max(scores, axis=0, keepdims=True) * LOG_SCALE
            grown = jnp.exp2(scores * LOG_SCALE - peak_here)
            total_here = jnp.sum(grown, axis=0, keepdims=True)
            delta_here = jnp.sum(grown * weight_grads, axis=0, keepdims=True)
            row = 3 * head
            peak = stats_ref[at, row : row + 1, :]
            new_peak = jnp.maximum(peak, peak_here)
            keep = jnp.exp2(peak - new_peak)
            add = jnp.exp2(peak_here - new_peak)
            stats_ref[at, row : row + 1, :] = new_peak
            stats_ref[at, row + 1 : row + 2, :] = (
                stats_ref[at, row + 1 : row + 2, :] * keep + total_here * add
            )
            stats_ref[at, row + 2 : row + 3, :] = (
                stats_ref[at, row + 2 : row + 3, :] * keep + delta_here * add
            )

    return step


def clear_stats(heads, slots, stats_ref):
    stats_ref[slots] = jnp.zeros_like(stats_ref[slots])
    for head in range(heads):
        stats_ref[slots, 3 * head : 3 * head + 1, :] = jnp.full(
            (slots.stop - slots.start, 1, BLOCK), LOWEST, jnp.float32
        )


def near_stats_kernel(
    heads, lane, place, lists, counts, km, ko, vm, vo, pm, po, xm, xo, stats, key_buf, value_buf, rows_buf, sem
):
    width = heads * HEAD_DIM
    fetch(
        key_copies(place, (km, ko, vm, vo), lane, width, key_buf, value_buf)
        + [(member, rows_buf.at[at]) for at, member in enumerate((pm, po, xm, xo))],
        sem,
    )
    clear_stats(heads, slice(0, 4), stats)
    step = stats_step(heads, 0, key_buf, value_buf, rows_buf, stats)
    for_live_pairs((place, lists, counts), 0, 4, step)


def far_stats_kernel(
    heads, lane, place, lists, counts, km, ko, vm, vo, ym, yo, near, stats, key_buf, value_buf, rows_buf, sem
):
    width = heads * HEAD_DIM
    fetch(
        key_copies(place, (km, ko, vm, vo), lane, width, key_buf, value_buf)
        + [(member, rows_buf.at[at]) for at, member in enumerate((ym, yo))]
        + [(near.at[pl.ds(0, 2)], stats.at[pl.ds(2, 2)])],
        sem,
    )
    clear_stats(heads, slice(0, 2), stats)
    step = stats_step(heads, 4, key_buf, value_buf, rows_buf, stats)
    for_live_pairs((place, lists, counts), 4, 6, step)


def merged(parts, slot, head):
    row = 3 * head
    peaks, totals, deltas = [], [], []
    for ref, base in parts:
        total = ref[base + slot, row + 1 : row + 2, :]
        peaks.append(jnp.where(total > 0.0, ref[base + slot, row : row + 1, :], LOWEST))
        totals.append(total)
        deltas.append(ref[base + slot, row + 2 : row + 3, :])
    peak = functools.reduce(jnp.maximum, peaks)
    factors = [jnp.exp2(member - peak) for member in peaks]
    total = sum(factor * member for factor, member in zip(factors, totals))
    delta = sum(factor * member for factor, member in zip(factors, deltas))
    return peak + jnp.log2(total), delta / total


def grads_kernel(
    heads, lane, place, lists, counts, km, ko, vm, vo, pm, po, xm, xo, ym, yo,
    near, far, from_partner, from_relay, from_other, from_end,
    own_out, partner_out, relayed_out, key_out, value_out,
    key_buf, value_buf, rows_buf, near_buf, far_buf, partner_buf, relay_buf, other_buf, end_buf,
    log_buf, query_acc, key_acc, value_acc, sem,
):
    width = heads * HEAD_DIM
    fetch(
        key_copies(place, (km, ko, vm, vo), lane, width, key_buf, value_buf)
        + [(member, rows_buf.at[at]) for at, member in enumerate((pm, po, xm, xo, ym, yo))]
        + [
            (near, near_buf),
            (far, far_buf),
            (from_partner, partner_buf),
            (from_relay, relay_buf),
            (from_other, other_buf),
            (from_end, end_buf),
        ],
        sem,
    )
    groups = (
        ((near_buf, 0), (partner_buf, 2), (other_buf, 0)),
        ((near_buf, 2), (partner_buf, 0), (end_buf, 0)),
        ((far_buf, 0), (other_buf, 2), (relay_buf, 2)),
    )
    for origin, parts in enumerate(groups):
        for slot in range(2):
            for head in range(heads):
                log_total, delta = merged(parts, slot, head)
                log_buf[2 * origin + slot, 2 * head : 2 * head + 1, :] = log_total
                log_buf[2 * origin + slot, 2 * head + 1 : 2 * head + 2, :] = delta
    query_acc[...] = jnp.zeros_like(query_acc)
    key_acc[...] = jnp.zeros_like(key_acc)
    value_acc[...] = jnp.zeros_like(value_acc)

    def step(query, key):
        for head in range(heads):
            lanes = slice(head * HEAD_DIM, (head + 1) * HEAD_DIM)
            key_block = key_buf[key, :, lanes]
            query_block = rows_buf[query, 0, :, lanes]
            grad_block = rows_buf[query, 1, :, lanes]
            scores = pair_rows(key_block, query_block)
            weights = jnp.exp2(scores * LOG_SCALE - log_buf[query, 2 * head : 2 * head + 1, :])
            weight_grads = pair_rows(value_buf[key, :, lanes], grad_block)
            score_low = (
                weights * (weight_grads - log_buf[query, 2 * head + 1 : 2 * head + 2, :])
            ).astype(jnp.bfloat16)
            value_acc[key, :, lanes] += product(weights.astype(jnp.bfloat16), grad_block)
            key_acc[key, :, lanes] += product(score_low, query_block)
            query_acc[query, lanes, :] += product(key_block.T, score_low)

    for_live_pairs((place, lists, counts), 0, 6, step)
    for head in range(heads):
        lanes = slice(head * HEAD_DIM, (head + 1) * HEAD_DIM)
        for slot in range(2):
            own_out[slot, :, lanes] = query_acc[slot, lanes, :].T * SCALE
            partner_out[slot, :, lanes] = query_acc[2 + slot, lanes, :].T * SCALE
            relayed_out[slot, :, lanes] = (query_acc[4 + slot, lanes, :].T * SCALE).astype(jnp.bfloat16)
    key_out[...] = (key_acc[...] * SCALE).astype(jnp.bfloat16)
    value_out[...] = value_acc[...].astype(jnp.bfloat16)


ANYWHERE = pl.BlockSpec(memory_space=pl.ANY)
SCALARS = pl.BlockSpec(memory_space=pltpu.SMEM)
FAST = pl.BlockSpec(memory_space=pltpu.VMEM)


def call(kernel, name, outs, n_any, scratch, n_copies, matmuls):
    pairs = 3 * 512 * 512
    return pl.pallas_call(
        kernel,
        out_shape=outs,
        in_specs=[SCALARS] * 3 + [ANYWHERE] * n_any,
        out_specs=jax.tree.map(lambda _: FAST, outs),
        scratch_shapes=scratch + [pltpu.SemaphoreType.DMA((n_copies,))],
        compiler_params=pltpu.CompilerParams(vmem_limit_bytes=VMEM_LIMIT),
        cost_estimate=pl.CostEstimate(
            flops=matmuls * 2 * pairs * 128, bytes_accessed=2 << 20, transcendentals=pairs
        ),
        name=name,
    )


def shards(query_rows, key_rows, value_rows, out_grad, key_blocks, block_counts):
    chips = lax.axis_size("seq")
    chip = lax.axis_index("seq")
    core = lax.axis_index("head")
    half = HEADS * HEAD_DIM // 2
    place = jnp.stack([chip, core, jnp.int32(chips)]).astype(jnp.int32)
    lists = key_blocks.reshape(-1)

    swap_pairs = [(0, 1), (1, 0)]
    partner_pairs = [(c, c ^ 1) for c in range(chips)]
    relay_pairs = [(c, c + 2) for c in range(0, chips - 2, 2)]
    relay_pairs += [(c, c - 2) for c in range(3, chips, 2)]
    back_pairs = [(b, a) for a, b in relay_pairs]
    other_pairs = [(c, c + 1) for c in range(1, chips - 1, 2)]
    other_pairs += [(b, a) for a, b in other_pairs]

    def swap(member):
        return lax.ppermute(member, "head", swap_pairs)

    def over(member, pairs):
        return lax.ppermute(member, "seq", pairs)

    def columns(member, which, lane, width):
        return lax.dynamic_slice_in_dim(member, which * half + lane, width, 1)

    lanes = []
    lane = 0
    for heads in CHUNKS:
        lanes.append((lane, heads))
        lane += heads * HEAD_DIM

    mine, other = [], []
    for lane, heads in lanes:
        width = heads * HEAD_DIM
        mine.append(
            jnp.stack([columns(query_rows, core, lane, width), columns(out_grad, core, lane, width)])
        )
        away = jnp.stack(
            [columns(query_rows, 1 - core, lane, width), columns(out_grad, 1 - core, lane, width)]
        )
        other.append(swap(away))
    key_other = swap(columns(key_rows, 1 - core, 0, half))
    value_other = swap(columns(value_rows, 1 - core, 0, half))
    keys = (key_rows, key_other, value_rows, value_other)

    results = []
    for at, (lane, heads) in enumerate(lanes):
        width = heads * HEAD_DIM
        stat_rows = -(-3 * heads // 8) * 8
        pm, po = mine[at], other[at]
        xm, xo = over(pm, partner_pairs), over(po, partner_pairs)
        ym, yo = over(xm, relay_pairs), over(xo, relay_pairs)
        stats_shape = jax.ShapeDtypeStruct((4, stat_rows, BLOCK), jnp.float32)
        buf = lambda count: pltpu.VMEM((count, 2, BLOCK, width), jnp.bfloat16)
        key_buf = pltpu.VMEM((2, BLOCK, width), jnp.bfloat16)
        stat_buf = pltpu.VMEM((4, stat_rows, BLOCK), jnp.float32)
        near = call(
            functools.partial(near_stats_kernel, heads, lane),
            "near_stats", stats_shape, 8, [key_buf, key_buf, buf(4)], 8, 2 * heads,
        )(place, lists, block_counts, *keys, pm, po, xm, xo)
        from_partner = over(near, partner_pairs)
        from_relay = over(near, relay_pairs)
        far = call(
            functools.partial(far_stats_kernel, heads, lane),
            "far_stats", stats_shape, 7, [key_buf, key_buf, buf(2)], 7, heads,
        )(place, lists, block_counts, *keys, ym, yo, near)
        from_other = over(far, other_pairs)
        from_end = over(far, back_pairs)
        full = jax.ShapeDtypeStruct((2, BLOCK, width), jnp.float32)
        low = jax.ShapeDtypeStruct((2, BLOCK, width), jnp.bfloat16)
        own, partner, relayed, key_grad, value_grad = call(
            functools.partial(grads_kernel, heads, lane),
            "grads", (full, full, low, low, low), 16,
            [key_buf, key_buf, buf(6)] + [stat_buf] * 6
            + [
                pltpu.VMEM((6, -(-2 * heads // 8) * 8, BLOCK), jnp.float32),
                pltpu.VMEM((6, width, BLOCK), jnp.float32),
                pltpu.VMEM((2, BLOCK, width), jnp.float32),
                pltpu.VMEM((2, BLOCK, width), jnp.float32),
            ],
            16, 10 * heads,
        )(
            place, lists, block_counts, *keys, pm, po, xm, xo, ym, yo,
            near, far, from_partner, from_relay, from_other, from_end,
        )
        back = over(relayed, back_pairs)
        home = over((partner + back.astype(jnp.float32)).astype(jnp.bfloat16), partner_pairs)
        query_grad = (own + home.astype(jnp.float32)).astype(jnp.bfloat16)
        results.append(
            [(member[0], swap(member[1])) for member in (query_grad, key_grad, value_grad)]
        )

    def assembled(parts):
        near_half = jnp.concatenate([part[0] for part in parts], axis=1)
        far_half = jnp.concatenate([part[1] for part in parts], axis=1)
        first = jnp.where(core == 0, near_half, far_half)
        second = jnp.where(core == 0, far_half, near_half)
        return jnp.concatenate([first, second], axis=1)

    return tuple(assembled([chunk[at] for chunk in results]) for at in range(3))


def solution(mesh):
    rows = P(("seq", "head"), None)
    return jax.shard_map(
        shards,
        mesh=mesh,
        in_specs=(rows, rows, rows, rows, P(), P()),
        out_specs=(rows, rows, rows),
        check_vma=False,
    )
```

```python
import functools
import math

import jax
import jax.numpy as jnp
from jax import lax
from jax.experimental import pallas as pl
from jax.experimental.pallas import tpu as pltpu
from jax.sharding import PartitionSpec as P

HEADS = 12
HEAD_DIM = 128
BLOCK = 512
MAXK = 3
GROUP = 4
SHARE = HEADS // GROUP
WINDOW = 2 * GROUP + 4
KEY_GROUPS = ((0,), (1, 2))
SCALE = HEAD_DIM ** -0.5
LOG_SCALE = SCALE * math.log2(math.e)
VMEM_LIMIT = 48 * 1024 * 1024

ANYWHERE = pl.BlockSpec(memory_space=pl.ANY)
SCALARS = pl.BlockSpec(memory_space=pltpu.SMEM)
FAST = pl.BlockSpec(memory_space=pltpu.VMEM)


def pair_rows(left, right):
    return lax.dot_general(
        left, right, (((1,), (1,)), ((), ())), preferred_element_type=jnp.float32
    )


def product(left, right):
    return jnp.dot(left, right, preferred_element_type=jnp.float32)


def copy_all(copies, sem):
    started = [
        pltpu.make_async_copy(source, target, sem.at[at])
        for at, (source, target) in enumerate(copies)
    ]
    for copy in started:
        copy.start()
    for copy in started:
        copy.wait()


def head_columns(spot, head):
    return pl.ds(pl.multiple_of((spot * SHARE + head) * HEAD_DIM, HEAD_DIM), HEAD_DIM)


def pack_kernel(heads, place, first, second, *rest):
    outs, sem = rest[:-1], rest[-1]
    spot = place[0] & (GROUP - 1)
    copies = []
    for away, out in enumerate(outs):
        for at, head in enumerate(heads):
            columns = head_columns(spot ^ away, head)
            copies.append((first.at[:, columns], out.at[2 * at]))
            copies.append((second.at[:, columns], out.at[2 * at + 1]))
    copy_all(copies, sem)


def pack(place, first, second, heads):
    out = jax.ShapeDtypeStruct((2 * len(heads), BLOCK, HEAD_DIM), first.dtype)
    return pl.pallas_call(
        functools.partial(pack_kernel, heads),
        out_shape=[out] * GROUP,
        in_specs=[SCALARS, ANYWHERE, ANYWHERE],
        out_specs=[ANYWHERE] * GROUP,
        scratch_shapes=[pltpu.SemaphoreType.DMA((2 * GROUP * len(heads),))],
        name="pack",
    )(place, first, second)


def grads_kernel(
    at, place, lists, counts,
    k0, k1, k2, k3, s0, s1, s2, s3, below, above, swapped_edge, q0, q1, q2, q3,
    d0, d1, d2, d3, near_out, far_out,
    keys, rows, sums, query_out, low, sem,
):
    chip, core = place[0], place[1]
    spot = chip & (GROUP - 1)
    first = 2 * (chip - spot) - 2
    pair = pl.ds(2 * at, 2)
    copies = []
    for away, (mine, other, row) in enumerate(zip((k0, k1, k2, k3), (s0, s1, s2, s3), (q0, q1, q2, q3))):
        block = 2 + 2 * (spot ^ away)
        copies.append((mine.at[pair], keys.at[block + core]))
        copies.append((other.at[pair], keys.at[block + 1 - core]))
        copies.append((row, rows.at[away]))
    copies.append((below.at[pair], keys.at[core]))
    copies.append((above.at[pair], keys.at[WINDOW - 2 + core]))
    copies.append((swapped_edge.at[pair], keys.at[jnp.where(core == 0, 1, WINDOW - 2)]))
    started = [
        pltpu.make_async_copy(source, target, sem.at[index])
        for index, (source, target) in enumerate(copies)
    ]
    for copy in started:
        copy.start()
    sums[...] = jnp.zeros_like(sums)
    for copy in started:
        copy.wait()

    def query_step(away, carry):
        block = first + 2 + 2 * (spot ^ away) + core
        count = counts[block]

        def live(slots):
            query_block, grad_block = rows[away, 0], rows[away, 1]
            places = [lists[block * MAXK + slot] - first for slot in range(slots)]
            scores = [pair_rows(keys[spot_at, 0], query_block) for spot_at in places]
            peak = functools.reduce(
                jnp.maximum, [jnp.max(member, axis=0, keepdims=True) for member in scores]
            )
            grown = [jnp.exp2(member * LOG_SCALE - peak * LOG_SCALE) for member in scores]
            weight_grads = [pair_rows(keys[spot_at, 1], grad_block) for spot_at in places]
            total = sum(jnp.sum(member, axis=0, keepdims=True) for member in grown)
            share = 1.0 / total
            delta = share * sum(
                jnp.sum(member * other, axis=0, keepdims=True)
                for member, other in zip(grown, weight_grads)
            )
            query_sum = None
            for spot_at, member, other in zip(places, grown, weight_grads):
                weights = member * share
                score_low = (weights * (other - delta)).astype(jnp.bfloat16)
                sums[spot_at, 1] += product(weights.astype(jnp.bfloat16), grad_block)
                sums[spot_at, 0] += product(score_low, query_block) * SCALE
                term = product(keys[spot_at, 0].T, score_low)
                query_sum = term if query_sum is None else query_sum + term
            query_out[away] = (query_sum * SCALE).T.astype(jnp.bfloat16)

        for slots in range(1, MAXK + 1):
            pl.when(count == slots)(functools.partial(live, slots))
        return carry

    lax.fori_loop(0, GROUP, query_step, 0)
    for index in range(GROUP + 1):
        low[index] = sums[2 * index + jnp.where(core == 0, 1, 2)].astype(jnp.bfloat16)
    copies = [(query_out.at[away], out) for away, out in enumerate((d0, d1, d2, d3))]
    copies += [(sums.at[2 * index + core], near_out.at[index]) for index in range(GROUP + 2)]
    copies.append((low, far_out))
    copy_all(copies, sem)


def grads(at, place, lists, counts, keys, swapped, below, above, swapped_edge, rows):
    block = (BLOCK, HEAD_DIM)
    outs = [jax.ShapeDtypeStruct(block, jnp.bfloat16)] * GROUP
    outs.append(jax.ShapeDtypeStruct((GROUP + 2, 2) + block, jnp.float32))
    outs.append(jax.ShapeDtypeStruct((GROUP + 1, 2) + block, jnp.bfloat16))
    pairs = 8 * BLOCK * BLOCK
    return pl.pallas_call(
        functools.partial(grads_kernel, at),
        out_shape=outs,
        in_specs=[SCALARS] * 3 + [ANYWHERE] * (3 * GROUP + 3),
        out_specs=[ANYWHERE] * len(outs),
        scratch_shapes=[
            pltpu.VMEM((WINDOW, 2) + block, jnp.bfloat16),
            pltpu.VMEM((GROUP, 2) + block, jnp.bfloat16),
            pltpu.VMEM((WINDOW, 2) + block, jnp.float32),
            pltpu.VMEM((GROUP,) + block, jnp.bfloat16),
            pltpu.VMEM((GROUP + 1, 2) + block, jnp.bfloat16),
            pltpu.SemaphoreType.DMA((3 * GROUP + 3,)),
        ],
        compiler_params=pltpu.CompilerParams(vmem_limit_bytes=VMEM_LIMIT),
        cost_estimate=pl.CostEstimate(
            flops=10 * pairs * HEAD_DIM, bytes_accessed=8 << 20, transcendentals=pairs
        ),
        name="grads",
    )(place, lists, counts, *keys, *swapped, below, above, swapped_edge, *rows)


def settle_kernel(place, near, far, below, above, o0, o1, o2, o3):
    spot, core = place[0] & (GROUP - 1), place[1]
    for away, out in enumerate((o0, o1, o2, o3)):
        index = spot ^ away
        total = near[index + 1] + far[index + core].astype(jnp.float32)
        total += jnp.where(index == 0, below[...].astype(jnp.float32), 0.0)
        total += jnp.where(index == GROUP - 1, above[...].astype(jnp.float32), 0.0)
        out[...] = total.astype(jnp.bfloat16)


def settle(place, near, far, below, above):
    out = jax.ShapeDtypeStruct((2, BLOCK, HEAD_DIM), jnp.bfloat16)
    return pl.pallas_call(
        settle_kernel,
        out_shape=[out] * GROUP,
        in_specs=[SCALARS] + [FAST] * 4,
        out_specs=[FAST] * GROUP,
        compiler_params=pltpu.CompilerParams(vmem_limit_bytes=VMEM_LIMIT),
        cost_estimate=pl.CostEstimate(flops=4 << 20, bytes_accessed=6 << 20, transcendentals=0),
        name="settle",
    )(place, near, far, below, above)


def gather_kernel(head, kept, place, *refs):
    queries, others = refs[:GROUP], refs[GROUP : 2 * GROUP]
    query_out, key_out, value_out = refs[2 * GROUP + kept : 2 * GROUP + kept + 3]
    sem = refs[-1]
    spot = place[0] & (GROUP - 1)
    copies = []
    for away in range(GROUP):
        columns = head_columns(spot ^ away, head)
        copies.append((queries[away], query_out.at[:, columns]))
        copies.append((others[away].at[0], key_out.at[:, columns]))
        copies.append((others[away].at[1], value_out.at[:, columns]))
    copy_all(copies, sem)


def gather(head, place, queries, others, so_far):
    kept = len(so_far)
    out = jax.ShapeDtypeStruct((BLOCK, HEADS * HEAD_DIM), jnp.bfloat16)
    return pl.pallas_call(
        functools.partial(gather_kernel, head, kept),
        out_shape=[out] * 3,
        in_specs=[SCALARS] + [ANYWHERE] * (2 * GROUP + kept),
        out_specs=[ANYWHERE] * 3,
        scratch_shapes=[pltpu.SemaphoreType.DMA((3 * GROUP,))],
        input_output_aliases={1 + 2 * GROUP + at: at for at in range(kept)},
        name="gather",
    )(place, *queries, *others, *so_far)


def shards(query_rows, key_rows, value_rows, out_grad, key_blocks, block_counts):
    chips = lax.axis_size("seq")
    chip = lax.axis_index("seq")
    core = lax.axis_index("head")
    spot = chip & (GROUP - 1)
    place = jnp.stack([chip, core]).astype(jnp.int32)
    lists = key_blocks.reshape(-1)

    def swap(member):
        return lax.ppermute(member, "head", [(0, 1), (1, 0)])

    def across(members):
        return [members[0]] + [
            lax.ppermute(members[away], "seq", [(c, c ^ away) for c in range(chips)])
            for away in range(1, GROUP)
        ]

    def upward(member):
        return lax.ppermute(member, "seq", [(c, c + GROUP) for c in range(chips - GROUP)])

    def downward(member):
        return lax.ppermute(member, "seq", [(c + GROUP, c) for c in range(chips - GROUP)])

    def pick(members, which):
        return lax.select_n(which, *members)

    where = {}
    windows = []
    for group, heads in enumerate(KEY_GROUPS):
        keys = across(pack(place, key_rows, value_rows, heads))
        from_below = upward(pick(keys, spot ^ (GROUP - 1)))
        from_above = downward(pick(keys, spot))
        swapped = [swap(member) for member in keys]
        swapped_edge = swap(jnp.where(core == 1, from_below, from_above))
        windows.append((keys, swapped, from_below, from_above, swapped_edge))
        for at, head in enumerate(heads):
            where[head] = (group, at)

    results = ()
    for head in range(SHARE):
        rows = across(pack(place, query_rows, out_grad, (head,)))
        group, at = where[head]
        *query_grads, near, far = grads(at, place, lists, block_counts, *windows[group], rows)
        query_grads = across(query_grads)
        far = swap(far)
        edge_low = near[0] + jnp.where(core == 1, far[0].astype(jnp.float32), 0.0)
        edge_high = near[GROUP + 1] + jnp.where(core == 0, far[GROUP].astype(jnp.float32), 0.0)
        from_above = downward(edge_low.astype(jnp.bfloat16))
        from_below = upward(edge_high.astype(jnp.bfloat16))
        others = across(settle(place, near, far, from_below, from_above))
        results = gather(head, place, query_grads, others, results)
    return tuple(results)


def solution(mesh):
    rows = P(("seq", "head"), None)
    return jax.shard_map(
        shards,
        mesh=mesh,
        in_specs=(rows, rows, rows, rows, P(), P()),
        out_specs=(rows, rows, rows),
        check_vma=False,
    )
```

```python
import functools
import math

import jax
import jax.numpy as jnp
from jax import lax
from jax.experimental import pallas as pl
from jax.experimental.pallas import tpu as pltpu
from jax.sharding import PartitionSpec as P

HEADS = 12
HEAD_DIM = 128
BLOCK = 512
MAXK = 3
GROUP = 4
SHARE = HEADS // GROUP
OWN = GROUP + 2
SEEN = OWN + GROUP + 1
FIRST, LAST = (0, 1), (2,)
SCALE = HEAD_DIM ** -0.5
LOG_SCALE = SCALE * math.log2(math.e)
COST_FLOPS, COST_BYTES = 1.15e+09, 3.00e+06
VMEM_LIMIT = 60 * 1024 * 1024

ANYWHERE = pl.BlockSpec(memory_space=pl.ANY)
SCALARS = pl.BlockSpec(memory_space=pltpu.SMEM)
FAST = pl.BlockSpec(memory_space=pltpu.VMEM)


def pair_rows(left, right):
    return lax.dot_general(
        left, right, (((1,), (1,)), ((), ())), preferred_element_type=jnp.float32
    )


def product(left, right):
    return jnp.dot(left, right, preferred_element_type=jnp.float32)


def copy_all(copies, sem):
    started = [
        pltpu.make_async_copy(source, target, sem.at[at])
        for at, (source, target) in enumerate(copies)
    ]
    for copy in started:
        copy.start()
    for copy in started:
        copy.wait()


def head_columns(spot, head):
    return pl.ds((spot * SHARE + head) * HEAD_DIM, HEAD_DIM)


def cost(microseconds):
    return pl.CostEstimate(
        flops=int(microseconds * COST_FLOPS),
        bytes_accessed=int(microseconds * COST_BYTES),
        transcendentals=0,
    )


def pack_kernel(heads, count, *refs):
    sources, out, sem = refs[:count], refs[-2], refs[-1]
    copies = []
    for spot in range(GROUP):
        for at, head in enumerate(heads):
            for index, source in enumerate(sources):
                target = out.at[spot, len(sources) * at + index]
                copies.append((source.at[:, head_columns(spot, head)], target))
    copy_all(copies, sem)


def pack(sources, heads, after=()):
    parts = len(sources) * len(heads)
    return pl.pallas_call(
        functools.partial(pack_kernel, heads, len(sources)),
        out_shape=jax.ShapeDtypeStruct((GROUP, parts, BLOCK, HEAD_DIM), sources[0].dtype),
        in_specs=[ANYWHERE] * (len(sources) + len(after)),
        out_specs=FAST,
        scratch_shapes=[pltpu.SemaphoreType.DMA((GROUP * parts,))],
        compiler_params=pltpu.CompilerParams(vmem_limit_bytes=VMEM_LIMIT),
        cost_estimate=cost(4),
        name="pack",
    )(*sources, *after)


def grads_kernel(heads, key_at, waited, place, lists, counts, *refs):
    near_keys, far_keys, below, above, cross, rows_in = refs[:6]
    refs = refs[6 + waited :]
    query_out, near_out, far_out, low_out, high_out, cross_out = refs[:6]
    keys, rows, sums, queries, rounded, sem = refs[6:]
    chip, core = place[0], place[1]
    here = chip & (GROUP - 1)
    first = 2 * (chip - here) - 2
    copies = []
    for head in range(heads):
        pair = pl.ds(key_at + 2 * head, 2)
        copies += [
            (near_keys.at[:, pair], keys.at[head, pl.ds(1, GROUP)]),
            (rows_in.at[:, pl.ds(2 * head, 2)], rows.at[head]),
            (far_keys.at[:, pair], keys.at[head, pl.ds(OWN, GROUP)]),
            (below.at[pair], keys.at[head, 0]),
            (above.at[pair], keys.at[head, OWN - 1]),
            (cross.at[pair], keys.at[head, SEEN - 1]),
        ]
    started = [
        pltpu.make_async_copy(source, target, sem.at[index])
        for index, (source, target) in enumerate(copies)
    ]
    for copy in started:
        copy.start()
    sums[...] = jnp.zeros_like(sums)
    for copy in started:
        copy.wait()

    def place_of(block):
        offset = block - first
        half = offset >> 1
        other = jnp.where((half >= 1) & (half <= GROUP), OWN - 1 + half, SEEN - 1)
        return jnp.where((offset & 1) == core, half, other)

    def query_step(spot, carry):
        block = first + 2 + 2 * spot + core
        count = counts[block]

        def live(slots, head):
            query_block, grad_block = rows[head, spot, 0], rows[head, spot, 1]
            places = [place_of(lists[block * MAXK + slot]) for slot in range(slots)]
            scores = [pair_rows(keys[head, at, 0], query_block) for at in places]
            peak = functools.reduce(
                jnp.maximum, [jnp.max(member, axis=0, keepdims=True) for member in scores]
            )
            grown = [jnp.exp2(member * LOG_SCALE - peak * LOG_SCALE) for member in scores]
            weight_grads = [pair_rows(keys[head, at, 1], grad_block) for at in places]
            total = sum(jnp.sum(member, axis=0, keepdims=True) for member in grown)
            share = 1.0 / total
            delta = share * sum(
                jnp.sum(member * other, axis=0, keepdims=True)
                for member, other in zip(grown, weight_grads)
            )
            query_sum = None
            for at, member, other in zip(places, grown, weight_grads):
                weights = member * share
                score_low = (weights * (other - delta)).astype(jnp.bfloat16)
                sums[head, at, 1] += product(weights.astype(jnp.bfloat16), grad_block)
                sums[head, at, 0] += product(score_low, query_block) * SCALE
                term = product(keys[head, at, 0].T, score_low)
                query_sum = term if query_sum is None else query_sum + term
            queries[spot, head] = (query_sum * SCALE).T.astype(jnp.bfloat16)

        def all_heads(slots):
            for head in range(heads):
                live(slots, head)

        for slots in range(1, MAXK + 1):
            pl.when(count == slots)(functools.partial(all_heads, slots))
        return carry

    lax.fori_loop(0, GROUP, query_step, 0)
    copies = [(queries, query_out)]
    for head in range(heads):
        copies.append((sums.at[head, pl.ds(1, GROUP)], near_out.at[:, head]))
        for index, spot in enumerate((*range(OWN, OWN + GROUP), 0, OWN - 1, SEEN - 1)):
            rounded[head, index] = sums[head, spot].astype(jnp.bfloat16)
        copies.append((rounded.at[head, pl.ds(0, GROUP)], far_out.at[:, head]))
        for index, out in enumerate((low_out, high_out, cross_out)):
            copies.append((rounded.at[head, GROUP + index], out.at[head]))
    copy_all(copies, sem)


def grads(heads, key_at, place, lists, counts, window, rows, after):
    block = (BLOCK, HEAD_DIM)
    edge = jax.ShapeDtypeStruct((heads, 2) + block, jnp.bfloat16)
    outs = [
        jax.ShapeDtypeStruct((GROUP, heads) + block, jnp.bfloat16),
        jax.ShapeDtypeStruct((GROUP, heads, 2) + block, jnp.float32),
        jax.ShapeDtypeStruct((GROUP, heads, 2) + block, jnp.bfloat16),
        edge,
        edge,
        edge,
    ]
    return pl.pallas_call(
        functools.partial(grads_kernel, heads, key_at, len(after)),
        out_shape=outs,
        in_specs=[SCALARS] * 3 + [ANYWHERE] * (6 + len(after)),
        out_specs=[ANYWHERE] * len(outs),
        scratch_shapes=[
            pltpu.VMEM((heads, SEEN, 2) + block, jnp.bfloat16),
            pltpu.VMEM((heads, GROUP, 2) + block, jnp.bfloat16),
            pltpu.VMEM((heads, SEEN, 2) + block, jnp.float32),
            pltpu.VMEM((GROUP, heads) + block, jnp.bfloat16),
            pltpu.VMEM((heads, GROUP + 3, 2) + block, jnp.bfloat16),
            pltpu.SemaphoreType.DMA((6 * heads,)),
        ],
        compiler_params=pltpu.CompilerParams(vmem_limit_bytes=VMEM_LIMIT),
        cost_estimate=cost(2 + 11 * heads),
        name="grads",
    )(place, lists, counts, *window, rows, *after)


def settle_kernel(waited, held, place, near, far, below, above, cross, *refs):
    count = len(refs) - 1 - waited - 2 * held
    queries, out = refs[:count], refs[count + held + waited]
    for source, target in zip(refs[count : count + held], refs[len(refs) - held :]):
        target[...] = source[...]
    spot, core = pl.program_id(0), place[1]
    out[0, :, :2] = (near[0] + far[0].astype(jnp.float32)).astype(jnp.bfloat16)
    if queries:
        out[0, :, 2] = queries[0][0]

    def more(*edges):
        total = near[0] + far[0].astype(jnp.float32)
        for edge in edges:
            total += edge[...].astype(jnp.float32)
        out[0, :, :2] = total.astype(jnp.bfloat16)

    pl.when((spot == 0) & (core == 0))(lambda: more(below, cross))
    pl.when((spot == 0) & (core == 1))(lambda: more(below))
    pl.when((spot == GROUP - 1) & (core == 0))(lambda: more(above))
    pl.when((spot == GROUP - 1) & (core == 1))(lambda: more(above, cross))


def settle(place, near, far, edges, queries, after, held=()):
    heads = near.shape[1]
    block = (BLOCK, HEAD_DIM)
    parts = 3 if queries else 2
    by_spot = pl.BlockSpec((1, heads, 2) + block, lambda spot: (spot, 0, 0, 0, 0))
    whole = pl.BlockSpec((heads, 2) + block, lambda spot: (0, 0, 0, 0))
    kept = pl.BlockSpec((1, 2) + block, lambda spot: (0, 0, 0, 0))
    query = pl.BlockSpec((1, heads) + block, lambda spot: (spot, 0, 0, 0))
    return pl.pallas_call(
        functools.partial(settle_kernel, len(after), len(held)),
        grid=(GROUP,),
        out_shape=[jax.ShapeDtypeStruct((GROUP, heads, parts) + block, jnp.bfloat16)]
        + [jax.ShapeDtypeStruct(member.shape, member.dtype) for member in held],
        in_specs=[SCALARS, by_spot, by_spot]
        + [whole] * 3
        + [query] * len(queries)
        + [kept] * len(held)
        + [ANYWHERE] * len(after),
        out_specs=[pl.BlockSpec((1, heads, parts) + block, lambda spot: (spot, 0, 0, 0, 0))]
        + [kept] * len(held),
        compiler_params=pltpu.CompilerParams(vmem_limit_bytes=VMEM_LIMIT),
        cost_estimate=cost(2 + 2 * heads),
        name="settle",
    )(place, near, far, *edges, *queries, *held, *after)


def gather_kernel(heads, members, *refs):
    pieces, outs, sem = refs[:members], refs[-4:-1], refs[-1]
    key_out, value_out, query_out = outs
    copies = []
    for spot in range(GROUP):
        for at, head in enumerate(heads):
            columns = head_columns(spot, head)
            others = pieces[0].at[spot, at]
            query = pieces[1].at[spot, at] if members == 2 else others.at[2]
            copies.append((others.at[0], key_out.at[:, columns]))
            copies.append((others.at[1], value_out.at[:, columns]))
            copies.append((query, query_out.at[:, columns]))
    copy_all(copies, sem)


def gather(heads, pieces, so_far):
    kept = len(so_far)
    out = jax.ShapeDtypeStruct((BLOCK, HEADS * HEAD_DIM), jnp.bfloat16)
    return pl.pallas_call(
        functools.partial(gather_kernel, heads, len(pieces)),
        out_shape=[out] * 3,
        in_specs=[FAST] * len(pieces) + [ANYWHERE] * kept,
        out_specs=[ANYWHERE] * 3,
        scratch_shapes=[pltpu.SemaphoreType.DMA((3 * GROUP * len(heads),))],
        input_output_aliases={len(pieces) + at: at for at in range(kept)},
        compiler_params=pltpu.CompilerParams(vmem_limit_bytes=VMEM_LIMIT),
        cost_estimate=cost(1 + 2 * len(heads)),
        name="gather",
    )(*pieces, *so_far)


def shards(query_rows, key_rows, value_rows, out_grad, key_blocks, block_counts):
    chips = lax.axis_size("seq")
    chip = lax.axis_index("seq")
    core = lax.axis_index("head")
    place = jnp.stack([chip, core]).astype(jnp.int32)
    lists = key_blocks.reshape(-1)
    groups = [list(range(c, c + GROUP)) for c in range(0, chips, GROUP)]

    def regroup(member):
        return lax.all_to_all(
            member, "seq", split_axis=0, concat_axis=0, axis_index_groups=groups, tiled=True
        )

    def swap(member):
        return lax.ppermute(member, "head", [(0, 1), (1, 0)])

    def upward(member):
        return lax.ppermute(member, "seq", [(c, c + GROUP) for c in range(chips - GROUP)])

    def downward(member):
        return lax.ppermute(member, "seq", [(c + GROUP, c) for c in range(chips - GROUP)])

    def crosswise(member):
        pairs = [(2 * c + 1, 2 * (c + GROUP)) for c in range(chips - GROUP)]
        return lax.ppermute(member, ("seq", "head"), pairs + [(b, a) for a, b in pairs])

    def edges_of(low, high, cross):
        return [upward(high), downward(low), crosswise(cross)]

    def window_of(keys):
        below, above = upward(keys[GROUP - 1]), downward(keys[0])
        return [keys, swap(keys), below, above, swap(jnp.where(core == 1, below, above))]

    window = window_of(regroup(pack((key_rows, value_rows), FIRST + LAST)))
    rows = regroup(pack((query_rows, out_grad), FIRST))
    last_rows = regroup(pack((query_rows, out_grad), LAST, window[1:]))
    queries, near, far, *edges = grads(
        len(FIRST), 0, place, lists, block_counts, window, rows, []
    )
    queries = regroup(queries)
    edges, far = edges_of(*edges), swap(far)
    last_queries, last_near, last_far, *last_edges = grads(
        len(LAST), 2 * len(FIRST), place, lists, block_counts, window, last_rows, [near]
    )
    last_far = swap(last_far)
    others, *last_edges = settle(place, near, far, edges, [], [last_near, queries], last_edges)
    last_edges = edges_of(*last_edges)
    last_others = settle(place, last_near, last_far, last_edges, [last_queries], [])[0]
    results = gather(FIRST, (regroup(others), queries), ())
    key_grad, value_grad, query_grad = gather(LAST, (regroup(last_others),), results)
    return query_grad, key_grad, value_grad


def solution(mesh):
    rows = P(("seq", "head"), None)
    return jax.shard_map(
        shards,
        mesh=mesh,
        in_specs=(rows, rows, rows, rows, P(), P()),
        out_specs=(rows, rows, rows),
        check_vma=False,
    )
```

```python
import functools
import math

import jax
import jax.numpy as jnp
from jax import lax
from jax.experimental import pallas as pl
from jax.experimental.pallas import tpu as pltpu
from jax.sharding import PartitionSpec as P

HEADS = 12
HEAD_DIM = 128
BLOCK = 512
MAXK = 3
GROUP = 4
SHARE = HEADS // GROUP
OWN = GROUP + 2
SEEN = OWN + GROUP + 1
CORES = 2
MEMBERS = GROUP * CORES
SCALE = HEAD_DIM ** -0.5
LOG_SCALE = SCALE * math.log2(math.e)
COST_FLOPS, COST_BYTES = 3.45e+09, 9.00e+06
VMEM_LIMIT = 60 * 1024 * 1024

ANYWHERE = pl.BlockSpec(memory_space=pl.ANY)
SCALARS = pl.BlockSpec(memory_space=pltpu.SMEM)
FAST = pl.BlockSpec(memory_space=pltpu.VMEM)


def pair_rows(left, right):
    return lax.dot_general(
        left, right, (((1,), (1,)), ((), ())), preferred_element_type=jnp.float32
    )


def product(left, right):
    return jnp.dot(left, right, preferred_element_type=jnp.float32)


def copy_all(copies, sem):
    started = [
        pltpu.make_async_copy(source, target, sem.at[at])
        for at, (source, target) in enumerate(copies)
    ]
    for copy in started:
        copy.start()
    for copy in started:
        copy.wait()


def head_columns(head):
    return pl.ds(head * HEAD_DIM, HEAD_DIM)


def cost(microseconds):
    return pl.CostEstimate(
        flops=int(microseconds * COST_FLOPS),
        bytes_accessed=int(microseconds * COST_BYTES),
        transcendentals=0,
    )


def pack_split_kernel(place, key_rows, value_rows, query_rows, out_grad, *refs):
    outs, sem = refs[:-1], refs[-1]
    here = place[0] & (GROUP - 1)
    copies = []
    for away, out in enumerate(outs):
        start = (SHARE * (here ^ away) + CORES) * HEAD_DIM
        columns = pl.ds(pl.multiple_of(start, HEAD_DIM), HEAD_DIM)
        for index, source in enumerate((key_rows, value_rows, query_rows, out_grad)):
            copies.append((source.at[:, columns], out.at[index]))
    copy_all(copies, sem)


def pack_split(place, sources):
    out = jax.ShapeDtypeStruct((len(sources), BLOCK, HEAD_DIM), jnp.bfloat16)
    return pl.pallas_call(
        pack_split_kernel,
        out_shape=[out] * GROUP,
        in_specs=[SCALARS] + [ANYWHERE] * len(sources),
        out_specs=[FAST] * GROUP,
        scratch_shapes=[pltpu.SemaphoreType.DMA((GROUP * len(sources),))],
        compiler_params=pltpu.CompilerParams(vmem_limit_bytes=VMEM_LIMIT),
        cost_estimate=cost(4),
        name="pack_split",
    )(place, *sources)


def pack_kernel(heads, *refs):
    sources, outs, sem = refs[:4], refs[4:6], refs[6]
    copies = []
    for at, head in enumerate(heads):
        for index, source in enumerate(sources):
            target = outs[index // 2].at[at, index % 2]
            copies.append((source.at[:, pl.ds(head * HEAD_DIM, HEAD_DIM)], target))
    copy_all(copies, sem)


def pack(sources, heads):
    out = jax.ShapeDtypeStruct((len(heads), 2, BLOCK, HEAD_DIM), jnp.bfloat16)
    return pl.pallas_call(
        functools.partial(pack_kernel, heads),
        out_shape=[out] * 2,
        in_specs=[ANYWHERE] * 4,
        out_specs=[FAST] * 2,
        scratch_shapes=[pltpu.SemaphoreType.DMA((4 * len(heads),))],
        compiler_params=pltpu.CompilerParams(vmem_limit_bytes=VMEM_LIMIT),
        cost_estimate=cost(6),
        name="pack",
    )(*sources)


def arrange_kernel(waited, place, *refs):
    members = refs[:GROUP]
    ordered, low, high, cross, sem = refs[GROUP + waited :]
    here, core = place[0] & (GROUP - 1), place[1]
    pair = pl.ds(0, 2)
    copies = []
    for away, member in enumerate(members):
        copies.append(pltpu.make_async_copy(member.at[pair], ordered.at[here ^ away], sem.at[away]))
    for copy in copies:
        copy.start()
    for copy in copies:
        copy.wait()
    low[0] = ordered[0]
    high[0] = ordered[GROUP - 1]
    cross[0] = ordered[core * (GROUP - 1)]


def arrange(place, members, after=()):
    block = (2, BLOCK, HEAD_DIM)
    edge = jax.ShapeDtypeStruct((1,) + block, jnp.bfloat16)
    return pl.pallas_call(
        functools.partial(arrange_kernel, len(after)),
        out_shape=[jax.ShapeDtypeStruct((GROUP,) + block, jnp.bfloat16), edge, edge, edge],
        in_specs=[SCALARS] + [ANYWHERE] * (GROUP + len(after)),
        out_specs=[FAST] * 4,
        scratch_shapes=[pltpu.SemaphoreType.DMA((GROUP,))],
        compiler_params=pltpu.CompilerParams(vmem_limit_bytes=VMEM_LIMIT),
        cost_estimate=cost(2.5),
        name="arrange",
    )(place, *members, *after)


def cut_kernel(pieces, place, member, *refs):
    outs, sem = refs[-1 - len(pieces) : -1], refs[-1]
    copies = []
    for piece, out in zip(pieces, outs):
        start, rows, parts = piece(place[1])
        copies.append((member.at[pl.ds(start, rows), pl.ds(0, parts)], out))
    copy_all(copies, sem)


def cut(place, member, pieces, after=()):
    shapes = [piece(0)[1:] + member.shape[2:] for piece in pieces]
    return pl.pallas_call(
        functools.partial(cut_kernel, pieces),
        out_shape=[jax.ShapeDtypeStruct(shape, member.dtype) for shape in shapes],
        in_specs=[SCALARS] + [ANYWHERE] * (1 + len(after)),
        out_specs=[FAST] * len(pieces),
        scratch_shapes=[pltpu.SemaphoreType.DMA((len(pieces),))],
        compiler_params=pltpu.CompilerParams(vmem_limit_bytes=VMEM_LIMIT),
        cost_estimate=cost(1.5),
        name="cut",
    )(place, member, *after)


def grads_core(first, place_of, spots, block_of, keys, rows, sums, queries, lists, counts):
    def query_step(spot, carry):
        block = block_of(spot)
        count = counts[block]

        def live(slots):
            query_block, grad_block = rows[spot, 0], rows[spot, 1]
            places = [place_of(lists[block * MAXK + slot] - first) for slot in range(slots)]
            scores = [pair_rows(keys[at, 0], query_block) for at in places]
            peak = functools.reduce(
                jnp.maximum, [jnp.max(member, axis=0, keepdims=True) for member in scores]
            )
            grown = [jnp.exp2(member * LOG_SCALE - peak * LOG_SCALE) for member in scores]
            weight_grads = [pair_rows(keys[at, 1], grad_block) for at in places]
            total = sum(jnp.sum(member, axis=0, keepdims=True) for member in grown)
            share = 1.0 / total
            delta = share * sum(
                jnp.sum(member * other, axis=0, keepdims=True)
                for member, other in zip(grown, weight_grads)
            )
            query_sum = None
            for at, member, other in zip(places, grown, weight_grads):
                weights = member * share
                score_low = (weights * (other - delta)).astype(jnp.bfloat16)
                sums[at, 1] += product(weights.astype(jnp.bfloat16), grad_block)
                sums[at, 0] += product(score_low, query_block) * SCALE
                term = product(keys[at, 0].T, score_low)
                query_sum = term if query_sum is None else query_sum + term
            queries[spot] = (query_sum * SCALE).T.astype(jnp.bfloat16)

        for slots in range(1, MAXK + 1):
            pl.when(count == slots)(functools.partial(live, slots))
        return carry

    lax.fori_loop(0, spots, query_step, 0)


def begin(copies, sem):
    started = [
        pltpu.make_async_copy(source, target, sem.at[at])
        for at, (source, target) in enumerate(copies)
    ]
    for copy in started:
        copy.start()
    return started


def split_grads_kernel(waited, place, lists, counts, *refs):
    member, swapped, below, above, cross = refs[:5]
    rows_in = refs[5 : 5 + GROUP]
    refs = refs[5 + GROUP + waited :]
    query_out, near_out, far_out, low_out, high_out, cross_out = refs[:6]
    keys, rows, sums, queries, rounded, sem = refs[6:]
    chip, core = place[0], place[1]
    first = 2 * (chip & ~(GROUP - 1)) - 2
    here = chip & (GROUP - 1)
    copies = begin(
        [(part.at[pl.ds(2, 2)], rows.at[here ^ away]) for away, part in enumerate(rows_in)]
        + [
            (member, keys.at[pl.ds(1, GROUP)]),
            (swapped, keys.at[pl.ds(OWN, GROUP)]),
            (below.at[0], keys.at[0]),
            (above.at[0], keys.at[OWN - 1]),
            (cross.at[0], keys.at[SEEN - 1]),
        ],
        sem,
    )
    sums[...] = jnp.zeros_like(sums)
    for copy in copies:
        copy.wait()

    def place_of(offset):
        half = offset >> 1
        other = jnp.where((half >= 1) & (half <= GROUP), OWN - 1 + half, SEEN - 1)
        return jnp.where((offset & 1) == core, half, other)

    def block_of(spot):
        return first + 2 + 2 * spot + core

    grads_core(first, place_of, GROUP, block_of, keys, rows, sums, queries, lists, counts)
    copies = begin([(queries, query_out), (sums.at[pl.ds(1, GROUP)], near_out)], sem)
    for index, spot in enumerate((*range(OWN, OWN + GROUP), 0, OWN - 1, SEEN - 1)):
        rounded[index] = sums[spot].astype(jnp.bfloat16)
    more = begin(
        [
            (rounded.at[pl.ds(0, GROUP)], far_out),
            (rounded.at[pl.ds(GROUP, 1)], low_out),
            (rounded.at[pl.ds(GROUP + 1, 1)], high_out),
            (rounded.at[pl.ds(GROUP + 2, 1)], cross_out),
        ],
        sem.at[pl.ds(2, 4)],
    )
    for copy in copies + more:
        copy.wait()


def split_grads(place, lists, counts, member, swapped, edges, rows, after=()):
    block = (BLOCK, HEAD_DIM)
    edge = jax.ShapeDtypeStruct((1, 2) + block, jnp.bfloat16)
    outs = [
        jax.ShapeDtypeStruct((GROUP,) + block, jnp.bfloat16),
        jax.ShapeDtypeStruct((GROUP, 2) + block, jnp.float32),
        jax.ShapeDtypeStruct((GROUP, 2) + block, jnp.bfloat16),
        edge,
        edge,
        edge,
    ]
    return pl.pallas_call(
        functools.partial(split_grads_kernel, len(after)),
        out_shape=outs,
        in_specs=[SCALARS] * 3 + [ANYWHERE] * (5 + GROUP + len(after)),
        out_specs=[ANYWHERE] * len(outs),
        scratch_shapes=[
            pltpu.VMEM((SEEN, 2) + block, jnp.bfloat16),
            pltpu.VMEM((GROUP, 2) + block, jnp.bfloat16),
            pltpu.VMEM((SEEN, 2) + block, jnp.float32),
            pltpu.VMEM((GROUP,) + block, jnp.bfloat16),
            pltpu.VMEM((GROUP + 3, 2) + block, jnp.bfloat16),
            pltpu.SemaphoreType.DMA((GROUP + 5,)),
        ],
        compiler_params=pltpu.CompilerParams(vmem_limit_bytes=VMEM_LIMIT),
        cost_estimate=cost(13),
        name="split_grads",
    )(place, lists, counts, member, swapped, *edges, *rows, *after)


def whole_grads_kernel(waited, place, lists, counts, *refs):
    member, below, above, rows_in = refs[:4]
    refs = refs[4 + waited :]
    query_out, sum_out, edge_out, low_out, high_out = refs[:5]
    keys, rows, sums, queries, rounded, sem = refs[5:]
    first = 2 * (place[0] & ~(GROUP - 1)) - 2
    copies = begin(
        [
            (member, keys.at[pl.ds(2, MEMBERS)]),
            (below, keys.at[pl.ds(0, 2)]),
            (above, keys.at[pl.ds(MEMBERS + 2, 2)]),
            (rows_in, rows),
        ],
        sem,
    )
    sums[...] = jnp.zeros_like(sums)
    for copy in copies:
        copy.wait()
    grads_core(
        first, lambda offset: offset, MEMBERS, lambda spot: first + 2 + spot,
        keys, rows, sums, queries, lists, counts,
    )
    copies = begin(
        [
            (queries, query_out),
            (sums.at[pl.ds(2, 2)], edge_out.at[pl.ds(0, 2)]),
            (sums.at[pl.ds(MEMBERS, 2)], edge_out.at[pl.ds(2, 2)]),
        ],
        sem,
    )
    rounded[...] = sums[...].astype(jnp.bfloat16)
    more = begin(
        [
            (rounded.at[pl.ds(2, MEMBERS)], sum_out),
            (rounded.at[pl.ds(0, 2)], low_out),
            (rounded.at[pl.ds(MEMBERS + 2, 2)], high_out),
        ],
        sem.at[pl.ds(3, 3)],
    )
    for copy in copies + more:
        copy.wait()


def whole_grads(place, lists, counts, member, edges, rows, after=()):
    block = (BLOCK, HEAD_DIM)
    edge = jax.ShapeDtypeStruct((2, 2) + block, jnp.bfloat16)
    outs = [
        jax.ShapeDtypeStruct((MEMBERS,) + block, jnp.bfloat16),
        jax.ShapeDtypeStruct((MEMBERS, 2) + block, jnp.bfloat16),
        jax.ShapeDtypeStruct((4, 2) + block, jnp.float32),
        edge,
        edge,
    ]
    return pl.pallas_call(
        functools.partial(whole_grads_kernel, len(after)),
        out_shape=outs,
        in_specs=[SCALARS] * 3 + [ANYWHERE] * (4 + len(after)),
        out_specs=[ANYWHERE] * len(outs),
        scratch_shapes=[
            pltpu.VMEM((MEMBERS + 4, 2) + block, jnp.bfloat16),
            pltpu.VMEM((MEMBERS, 2) + block, jnp.bfloat16),
            pltpu.VMEM((MEMBERS + 4, 2) + block, jnp.float32),
            pltpu.VMEM((MEMBERS,) + block, jnp.bfloat16),
            pltpu.VMEM((MEMBERS + 4, 2) + block, jnp.bfloat16),
            pltpu.SemaphoreType.DMA((6,)),
        ],
        compiler_params=pltpu.CompilerParams(vmem_limit_bytes=VMEM_LIMIT),
        cost_estimate=cost(22),
        name="whole_grads",
    )(place, lists, counts, member, *edges, rows, *after)


def split_settle_kernel(waited, place, near, far, below, above, cross, queries, *refs):
    outs = refs[waited:]
    here, core = place[0] & (GROUP - 1), place[1]
    for away, out in enumerate(outs):
        spot = here ^ away
        out[:2] = (near[spot] + far[spot].astype(jnp.float32)).astype(jnp.bfloat16)
        out[2] = queries[spot]

        def more(out, spot, *edges):
            total = near[spot] + far[spot].astype(jnp.float32)
            for edge in edges:
                total += edge[0].astype(jnp.float32)
            out[:2] = total.astype(jnp.bfloat16)

        low, high = spot == 0, spot == GROUP - 1
        pl.when(low & (core == 0))(functools.partial(more, out, spot, below, cross))
        pl.when(low & (core == 1))(functools.partial(more, out, spot, below))
        pl.when(high & (core == 0))(functools.partial(more, out, spot, above))
        pl.when(high & (core == 1))(functools.partial(more, out, spot, above, cross))


def split_settle(place, near, far, edges, queries, after=()):
    out = jax.ShapeDtypeStruct((3, BLOCK, HEAD_DIM), jnp.bfloat16)
    return pl.pallas_call(
        functools.partial(split_settle_kernel, len(after)),
        out_shape=[out] * GROUP,
        in_specs=[SCALARS] + [FAST] * 6 + [ANYWHERE] * len(after),
        out_specs=[FAST] * GROUP,
        compiler_params=pltpu.CompilerParams(vmem_limit_bytes=VMEM_LIMIT),
        cost_estimate=cost(4),
        name="split_settle",
    )(place, near, far, *edges, queries, *after)


def whole_settle_kernel(near, below, above, summed, *refs):
    out = refs[-1]
    at = pl.program_id(0)

    @pl.when(at < 2)
    def _():
        out[...] = (near[...] + below[...].astype(jnp.float32)).astype(jnp.bfloat16)

    @pl.when(at >= 2)
    def _():
        out[...] = (near[...] + above[...].astype(jnp.float32)).astype(jnp.bfloat16)


def whole_settle(near, below, above, summed, after=()):
    one = (1, 2, BLOCK, HEAD_DIM)
    return pl.pallas_call(
        whole_settle_kernel,
        grid=(4,),
        out_shape=jax.ShapeDtypeStruct(summed.shape, summed.dtype),
        in_specs=[
            pl.BlockSpec(one, lambda at: (at, 0, 0, 0)),
            pl.BlockSpec(one, lambda at: (jnp.minimum(at, 1), 0, 0, 0)),
            pl.BlockSpec(one, lambda at: (jnp.maximum(at - 2, 0), 0, 0, 0)),
        ]
        + [ANYWHERE] * (1 + len(after)),
        out_specs=pl.BlockSpec(
            one, lambda at: (jnp.where(at < 2, at, MEMBERS - 4 + at), 0, 0, 0)
        ),
        input_output_aliases={3: 0},
        compiler_params=pltpu.CompilerParams(vmem_limit_bytes=VMEM_LIMIT),
        cost_estimate=cost(3),
        name="whole_settle",
    )(near, below, above, summed, *after)


def gather_split_kernel(place, *refs):
    pieces, outs, sem = refs[:GROUP], refs[GROUP:-1], refs[-1]
    here = place[0] & (GROUP - 1)
    copies = []
    for away, piece in enumerate(pieces):
        start = (SHARE * (here ^ away) + CORES) * HEAD_DIM
        columns = pl.ds(pl.multiple_of(start, HEAD_DIM), HEAD_DIM)
        for index, out in enumerate(outs):
            copies.append((piece.at[index], out.at[:, columns]))
    copy_all(copies, sem)


def gather_split(place, pieces):
    return pl.pallas_call(
        gather_split_kernel,
        out_shape=[jax.ShapeDtypeStruct((BLOCK, HEADS * HEAD_DIM), jnp.bfloat16)] * 3,
        in_specs=[SCALARS] + [FAST] * GROUP,
        out_specs=[ANYWHERE] * 3,
        scratch_shapes=[pltpu.SemaphoreType.DMA((3 * GROUP,))],
        compiler_params=pltpu.CompilerParams(vmem_limit_bytes=VMEM_LIMIT),
        cost_estimate=cost(3),
        name="gather_split",
    )(place, *pieces)


def gather_kernel(columns, count, *refs):
    outs, sem = refs[-1 - count : -1], refs[-1]
    copies = []
    for at, head in enumerate(columns):
        for index in range(count):
            copies.append((refs[0].at[at, index], outs[index].at[:, head_columns(head)]))
    copy_all(copies, sem)


def gather(columns, pieces, so_far=()):
    count, kept = pieces.shape[1], len(so_far)
    return pl.pallas_call(
        functools.partial(gather_kernel, columns, count),
        out_shape=[jax.ShapeDtypeStruct((BLOCK, HEADS * HEAD_DIM), jnp.bfloat16)] * count,
        in_specs=[FAST] + [ANYWHERE] * kept,
        out_specs=[ANYWHERE] * count,
        scratch_shapes=[pltpu.SemaphoreType.DMA((count * len(columns),))],
        input_output_aliases={1 + at: at for at in range(kept)},
        compiler_params=pltpu.CompilerParams(vmem_limit_bytes=VMEM_LIMIT),
        cost_estimate=cost(3),
        name="gather",
    )(pieces, *so_far)


def shards(query_rows, key_rows, value_rows, out_grad, key_blocks, block_counts):
    chips = lax.axis_size("seq")
    chip = lax.axis_index("seq")
    core = lax.axis_index("head")
    place = jnp.stack([chip, core]).astype(jnp.int32)
    lists = key_blocks.reshape(-1)
    wide = [list(range(d, d + MEMBERS)) for d in range(0, CORES * chips, MEMBERS)]
    whole_heads = [SHARE * spot + at for spot in range(GROUP) for at in range(CORES)]

    def across(members):
        return [members[0]] + [
            lax.ppermute(members[away], "seq", [(c, c ^ away) for c in range(chips)])
            for away in range(1, GROUP)
        ]

    def regroup_wide(member):
        return lax.all_to_all(
            member, ("seq", "head"), split_axis=0, concat_axis=0, axis_index_groups=wide, tiled=True
        )

    def swap(member):
        return lax.ppermute(member, "head", [(0, 1), (1, 0)])

    def upward(member):
        return lax.ppermute(member, "seq", [(c, c + GROUP) for c in range(chips - GROUP)])

    def downward(member):
        return lax.ppermute(member, "seq", [(c + GROUP, c) for c in range(chips - GROUP)])

    def crosswise(member):
        pairs = [(2 * c + 1, 2 * (c + GROUP)) for c in range(chips - GROUP)]
        return lax.ppermute(member, ("seq", "head"), pairs + [(b, a) for a, b in pairs])

    sources = (key_rows, value_rows, query_rows, out_grad)
    split = across(pack_split(place, sources))
    keys, rows = pack(sources, whole_heads)
    keys = regroup_wide(keys)
    rows = regroup_wide(rows)
    ordered, low, high, cross = arrange(place, split, [])
    edges = [upward(high), downward(low), crosswise(cross)]
    queries, near, far, low, high, cross = split_grads(
        place, lists, block_counts, ordered, swap(ordered), edges, split, []
    )
    edges, far = [upward(high), downward(low), crosswise(cross)], swap(far)
    low, high = cut(
        place,
        keys,
        [lambda core: (0, 2, 2), lambda core: (MEMBERS - 2, 2, 2)],
        [],
    )
    whole_edges = [upward(high), downward(low)]
    split_done = split_settle(place, near, far, edges, queries, [])
    split_out = across(split_done)
    whole_queries, whole_sums, whole_near, low, high = whole_grads(
        place, lists, block_counts, keys, whole_edges, rows, []
    )
    below, above = upward(high), downward(low)
    whole_queries = regroup_wide(whole_queries)
    whole_sums = whole_settle(whole_near, below, above, whole_sums, [whole_queries])
    whole_out = regroup_wide(whole_sums)
    key_grad, value_grad, query_grad = gather_split(place, split_out)
    (query_grad,) = gather(whole_heads, whole_queries[:, None], (query_grad,))
    key_grad, value_grad = gather(whole_heads, whole_out, (key_grad, value_grad))
    return query_grad, key_grad, value_grad


def solution(mesh):
    rows = P(("seq", "head"), None)
    return jax.shard_map(
        shards,
        mesh=mesh,
        in_specs=(rows, rows, rows, rows, P(), P()),
        out_specs=(rows, rows, rows),
        check_vma=False,
    )
```

```python
import functools
import math

import jax
import jax.numpy as jnp
from jax import lax
from jax.experimental import pallas as pl
from jax.experimental.pallas import tpu as pltpu
from jax.sharding import PartitionSpec as P

HEADS = 12
HEAD_DIM = 128
BLOCK = 512
MAXK = 3
GROUP = 4
SHARE = HEADS // GROUP
OWN = GROUP + 2
SEEN = OWN + GROUP + 1
CORES = 2
MEMBERS = GROUP * CORES
SCALE = HEAD_DIM ** -0.5
LOG_SCALE = SCALE * math.log2(math.e)
COST_FLOPS, COST_BYTES = 3.45e+09, 9.00e+06
VMEM_LIMIT = 60 * 1024 * 1024

ANYWHERE = pl.BlockSpec(memory_space=pl.ANY)
SCALARS = pl.BlockSpec(memory_space=pltpu.SMEM)
FAST = pl.BlockSpec(memory_space=pltpu.VMEM)


def pair_rows(left, right):
    return lax.dot_general(
        left, right, (((1,), (1,)), ((), ())), preferred_element_type=jnp.float32
    )


def product(left, right):
    return jnp.dot(left, right, preferred_element_type=jnp.float32)


def copy_all(copies, sem):
    started = [
        pltpu.make_async_copy(source, target, sem.at[at])
        for at, (source, target) in enumerate(copies)
    ]
    for copy in started:
        copy.start()
    for copy in started:
        copy.wait()


def head_columns(head):
    return pl.ds(head * HEAD_DIM, HEAD_DIM)


def cost(microseconds):
    return pl.CostEstimate(
        flops=int(microseconds * COST_FLOPS),
        bytes_accessed=int(microseconds * COST_BYTES),
        transcendentals=0,
    )


def pack_split_kernel(place, key_rows, value_rows, query_rows, out_grad, *refs):
    outs, sem = refs[:-1], refs[-1]
    here = place[0] & (GROUP - 1)
    copies = []
    for away, out in enumerate(outs):
        start = (SHARE * (here ^ away) + CORES) * HEAD_DIM
        columns = pl.ds(pl.multiple_of(start, HEAD_DIM), HEAD_DIM)
        for index, source in enumerate((key_rows, value_rows, query_rows, out_grad)):
            copies.append((source.at[:, columns], out.at[index]))
    copy_all(copies, sem)


def pack_split(place, sources):
    out = jax.ShapeDtypeStruct((len(sources), BLOCK, HEAD_DIM), jnp.bfloat16)
    return pl.pallas_call(
        pack_split_kernel,
        out_shape=[out] * GROUP,
        in_specs=[SCALARS] + [ANYWHERE] * len(sources),
        out_specs=[FAST] * GROUP,
        scratch_shapes=[pltpu.SemaphoreType.DMA((GROUP * len(sources),))],
        compiler_params=pltpu.CompilerParams(vmem_limit_bytes=VMEM_LIMIT),
        cost_estimate=cost(4),
        name="pack_split",
    )(place, *sources)


def pack_kernel(heads, *refs):
    sources, outs, sem = refs[:4], refs[4:6], refs[6]
    copies = []
    for at, head in enumerate(heads):
        for index, source in enumerate(sources):
            target = outs[index // 2].at[at, index % 2]
            copies.append((source.at[:, pl.ds(head * HEAD_DIM, HEAD_DIM)], target))
    copy_all(copies, sem)


def pack(sources, heads):
    out = jax.ShapeDtypeStruct((len(heads), 2, BLOCK, HEAD_DIM), jnp.bfloat16)
    return pl.pallas_call(
        functools.partial(pack_kernel, heads),
        out_shape=[out] * 2,
        in_specs=[ANYWHERE] * 4,
        out_specs=[FAST] * 2,
        scratch_shapes=[pltpu.SemaphoreType.DMA((4 * len(heads),))],
        compiler_params=pltpu.CompilerParams(vmem_limit_bytes=VMEM_LIMIT),
        cost_estimate=cost(6),
        name="pack",
    )(*sources)


def arrange_kernel(waited, place, *refs):
    members = refs[:GROUP]
    ordered, low, high, cross, sem = refs[GROUP + waited :]
    here, core = place[0] & (GROUP - 1), place[1]
    pair = pl.ds(0, 2)
    copies = []
    for away, member in enumerate(members):
        copies.append(pltpu.make_async_copy(member.at[pair], ordered.at[here ^ away], sem.at[away]))
    for copy in copies:
        copy.start()
    for copy in copies:
        copy.wait()
    low[0] = ordered[0]
    high[0] = ordered[GROUP - 1]
    cross[0] = ordered[core * (GROUP - 1)]


def arrange(place, members, after=()):
    block = (2, BLOCK, HEAD_DIM)
    edge = jax.ShapeDtypeStruct((1,) + block, jnp.bfloat16)
    return pl.pallas_call(
        functools.partial(arrange_kernel, len(after)),
        out_shape=[jax.ShapeDtypeStruct((GROUP,) + block, jnp.bfloat16), edge, edge, edge],
        in_specs=[SCALARS] + [ANYWHERE] * (GROUP + len(after)),
        out_specs=[FAST] * 4,
        scratch_shapes=[pltpu.SemaphoreType.DMA((GROUP,))],
        compiler_params=pltpu.CompilerParams(vmem_limit_bytes=16 << 20),
        cost_estimate=cost(2.5),
        name="arrange",
    )(place, *members, *after)


def cut_kernel(pieces, place, member, *refs):
    outs, sem = refs[-1 - len(pieces) : -1], refs[-1]
    copies = []
    for piece, out in zip(pieces, outs):
        start, rows, parts = piece(place[1])
        copies.append((member.at[pl.ds(start, rows), pl.ds(0, parts)], out))
    copy_all(copies, sem)


def cut(place, member, pieces, after=()):
    shapes = [piece(0)[1:] + member.shape[2:] for piece in pieces]
    return pl.pallas_call(
        functools.partial(cut_kernel, pieces),
        out_shape=[jax.ShapeDtypeStruct(shape, member.dtype) for shape in shapes],
        in_specs=[SCALARS] + [ANYWHERE] * (1 + len(after)),
        out_specs=[FAST] * len(pieces),
        scratch_shapes=[pltpu.SemaphoreType.DMA((len(pieces),))],
        compiler_params=pltpu.CompilerParams(vmem_limit_bytes=16 << 20),
        cost_estimate=cost(1.5),
        name="cut",
    )(place, member, *after)


def grads_core(first, place_of, spots, block_of, keys, rows, sums, queries, lists, counts):
    def query_step(spot, carry):
        block = block_of(spot)
        count = counts[block]

        def live(slots):
            query_block, grad_block = rows[spot, 0], rows[spot, 1]
            places = [place_of(lists[block * MAXK + slot] - first) for slot in range(slots)]
            scores = [pair_rows(keys[at, 0], query_block) for at in places]
            peak = functools.reduce(
                jnp.maximum, [jnp.max(member, axis=0, keepdims=True) for member in scores]
            )
            grown = [jnp.exp2(member * LOG_SCALE - peak * LOG_SCALE) for member in scores]
            weight_grads = [pair_rows(keys[at, 1], grad_block) for at in places]
            total = sum(jnp.sum(member, axis=0, keepdims=True) for member in grown)
            share = 1.0 / total
            delta = share * sum(
                jnp.sum(member * other, axis=0, keepdims=True)
                for member, other in zip(grown, weight_grads)
            )
            query_sum = None
            for at, member, other in zip(places, grown, weight_grads):
                weights = member * share
                score_low = (weights * (other - delta)).astype(jnp.bfloat16)
                sums[at, 1] += product(weights.astype(jnp.bfloat16), grad_block)
                sums[at, 0] += product(score_low, query_block) * SCALE
                term = product(keys[at, 0].T, score_low)
                query_sum = term if query_sum is None else query_sum + term
            queries[spot] = (query_sum * SCALE).T.astype(jnp.bfloat16)

        for slots in range(1, MAXK + 1):
            pl.when(count == slots)(functools.partial(live, slots))
        return carry

    lax.fori_loop(0, spots, query_step, 0)


def begin(copies, sem):
    started = [
        pltpu.make_async_copy(source, target, sem.at[at])
        for at, (source, target) in enumerate(copies)
    ]
    for copy in started:
        copy.start()
    return started


def split_grads_kernel(waited, place, lists, counts, *refs):
    member, swapped, below, above, cross = refs[:5]
    rows_in = refs[5 : 5 + GROUP]
    refs = refs[5 + GROUP + waited :]
    query_out, near_out, far_out, low_out, high_out, cross_out = refs[:6]
    keys, rows, sums, queries, rounded, sem = refs[6:]
    chip, core = place[0], place[1]
    first = 2 * (chip & ~(GROUP - 1)) - 2
    here = chip & (GROUP - 1)
    copies = begin(
        [(part.at[pl.ds(2, 2)], rows.at[here ^ away]) for away, part in enumerate(rows_in)]
        + [
            (member, keys.at[pl.ds(1, GROUP)]),
            (swapped, keys.at[pl.ds(OWN, GROUP)]),
            (below.at[0], keys.at[0]),
            (above.at[0], keys.at[OWN - 1]),
            (cross.at[0], keys.at[SEEN - 1]),
        ],
        sem,
    )
    sums[...] = jnp.zeros_like(sums)
    for copy in copies:
        copy.wait()

    def place_of(offset):
        half = offset >> 1
        other = jnp.where((half >= 1) & (half <= GROUP), OWN - 1 + half, SEEN - 1)
        return jnp.where((offset & 1) == core, half, other)

    def block_of(spot):
        return first + 2 + 2 * spot + core

    grads_core(first, place_of, GROUP, block_of, keys, rows, sums, queries, lists, counts)
    copies = begin([(queries, query_out), (sums.at[pl.ds(1, GROUP)], near_out)], sem)
    for index, spot in enumerate((*range(OWN, OWN + GROUP), 0, OWN - 1, SEEN - 1)):
        rounded[index] = sums[spot].astype(jnp.bfloat16)
    more = begin(
        [
            (rounded.at[pl.ds(0, GROUP)], far_out),
            (rounded.at[pl.ds(GROUP, 1)], low_out),
            (rounded.at[pl.ds(GROUP + 1, 1)], high_out),
            (rounded.at[pl.ds(GROUP + 2, 1)], cross_out),
        ],
        sem.at[pl.ds(2, 4)],
    )
    for copy in copies + more:
        copy.wait()


def split_grads(place, lists, counts, member, swapped, edges, rows, after=()):
    block = (BLOCK, HEAD_DIM)
    edge = jax.ShapeDtypeStruct((1, 2) + block, jnp.bfloat16)
    outs = [
        jax.ShapeDtypeStruct((GROUP,) + block, jnp.bfloat16),
        jax.ShapeDtypeStruct((GROUP, 2) + block, jnp.float32),
        jax.ShapeDtypeStruct((GROUP, 2) + block, jnp.bfloat16),
        edge,
        edge,
        edge,
    ]
    return pl.pallas_call(
        functools.partial(split_grads_kernel, len(after)),
        out_shape=outs,
        in_specs=[SCALARS] * 3 + [ANYWHERE] * (5 + GROUP + len(after)),
        out_specs=[ANYWHERE] * len(outs),
        scratch_shapes=[
            pltpu.VMEM((SEEN, 2) + block, jnp.bfloat16),
            pltpu.VMEM((GROUP, 2) + block, jnp.bfloat16),
            pltpu.VMEM((SEEN, 2) + block, jnp.float32),
            pltpu.VMEM((GROUP,) + block, jnp.bfloat16),
            pltpu.VMEM((GROUP + 3, 2) + block, jnp.bfloat16),
            pltpu.SemaphoreType.DMA((GROUP + 5,)),
        ],
        compiler_params=pltpu.CompilerParams(vmem_limit_bytes=VMEM_LIMIT),
        cost_estimate=cost(13),
        name="split_grads",
    )(place, lists, counts, member, swapped, *edges, *rows, *after)


def whole_grads_kernel(waited, place, lists, counts, *refs):
    member, below, above, rows_in = refs[:4]
    refs = refs[4 + waited :]
    query_out, sum_out, edge_out, low_out, high_out = refs[:5]
    keys, rows, sums, queries, rounded, sem = refs[5:]
    first = 2 * (place[0] & ~(GROUP - 1)) - 2
    copies = begin(
        [
            (member, keys.at[pl.ds(2, MEMBERS)]),
            (below, keys.at[pl.ds(0, 2)]),
            (above, keys.at[pl.ds(MEMBERS + 2, 2)]),
            (rows_in, rows),
        ],
        sem,
    )
    sums[...] = jnp.zeros_like(sums)
    for copy in copies:
        copy.wait()
    grads_core(
        first, lambda offset: offset, MEMBERS, lambda spot: first + 2 + spot,
        keys, rows, sums, queries, lists, counts,
    )
    copies = begin(
        [
            (queries, query_out),
            (sums.at[pl.ds(2, 2)], edge_out.at[pl.ds(0, 2)]),
            (sums.at[pl.ds(MEMBERS, 2)], edge_out.at[pl.ds(2, 2)]),
        ],
        sem,
    )
    rounded[...] = sums[...].astype(jnp.bfloat16)
    more = begin(
        [
            (rounded.at[pl.ds(2, MEMBERS)], sum_out),
            (rounded.at[pl.ds(0, 2)], low_out),
            (rounded.at[pl.ds(MEMBERS + 2, 2)], high_out),
        ],
        sem.at[pl.ds(3, 3)],
    )
    for copy in copies + more:
        copy.wait()


def whole_grads(place, lists, counts, member, edges, rows, after=()):
    block = (BLOCK, HEAD_DIM)
    edge = jax.ShapeDtypeStruct((2, 2) + block, jnp.bfloat16)
    outs = [
        jax.ShapeDtypeStruct((MEMBERS,) + block, jnp.bfloat16),
        jax.ShapeDtypeStruct((MEMBERS, 2) + block, jnp.bfloat16),
        jax.ShapeDtypeStruct((4, 2) + block, jnp.float32),
        edge,
        edge,
    ]
    return pl.pallas_call(
        functools.partial(whole_grads_kernel, len(after)),
        out_shape=outs,
        in_specs=[SCALARS] * 3 + [ANYWHERE] * (4 + len(after)),
        out_specs=[ANYWHERE] * len(outs),
        scratch_shapes=[
            pltpu.VMEM((MEMBERS + 4, 2) + block, jnp.bfloat16),
            pltpu.VMEM((MEMBERS, 2) + block, jnp.bfloat16),
            pltpu.VMEM((MEMBERS + 4, 2) + block, jnp.float32),
            pltpu.VMEM((MEMBERS,) + block, jnp.bfloat16),
            pltpu.VMEM((MEMBERS + 4, 2) + block, jnp.bfloat16),
            pltpu.SemaphoreType.DMA((6,)),
        ],
        compiler_params=pltpu.CompilerParams(vmem_limit_bytes=VMEM_LIMIT),
        cost_estimate=cost(22),
        name="whole_grads",
    )(place, lists, counts, member, *edges, rows, *after)


def split_settle_kernel(waited, place, near, far, below, above, cross, queries, *refs):
    outs = refs[waited:]
    here, core = place[0] & (GROUP - 1), place[1]
    for away, out in enumerate(outs):
        spot = here ^ away
        out[:2] = (near[spot] + far[spot].astype(jnp.float32)).astype(jnp.bfloat16)
        out[2] = queries[spot]

        def more(out, spot, *edges):
            total = near[spot] + far[spot].astype(jnp.float32)
            for edge in edges:
                total += edge[0].astype(jnp.float32)
            out[:2] = total.astype(jnp.bfloat16)

        low, high = spot == 0, spot == GROUP - 1
        pl.when(low & (core == 0))(functools.partial(more, out, spot, below, cross))
        pl.when(low & (core == 1))(functools.partial(more, out, spot, below))
        pl.when(high & (core == 0))(functools.partial(more, out, spot, above))
        pl.when(high & (core == 1))(functools.partial(more, out, spot, above, cross))


def split_settle(place, near, far, edges, queries, after=()):
    out = jax.ShapeDtypeStruct((3, BLOCK, HEAD_DIM), jnp.bfloat16)
    return pl.pallas_call(
        functools.partial(split_settle_kernel, len(after)),
        out_shape=[out] * GROUP,
        in_specs=[SCALARS] + [FAST] * 6 + [ANYWHERE] * len(after),
        out_specs=[FAST] * GROUP,
        compiler_params=pltpu.CompilerParams(vmem_limit_bytes=16 << 20),
        cost_estimate=cost(4),
        name="split_settle",
    )(place, near, far, *edges, queries, *after)


def whole_settle_kernel(near, below, above, summed, *refs):
    out = refs[-1]
    at = pl.program_id(0)

    @pl.when(at < 2)
    def _():
        out[...] = (near[...] + below[...].astype(jnp.float32)).astype(jnp.bfloat16)

    @pl.when(at >= 2)
    def _():
        out[...] = (near[...] + above[...].astype(jnp.float32)).astype(jnp.bfloat16)


def whole_settle(near, below, above, summed, after=()):
    one = (1, 2, BLOCK, HEAD_DIM)
    return pl.pallas_call(
        whole_settle_kernel,
        grid=(4,),
        out_shape=jax.ShapeDtypeStruct(summed.shape, summed.dtype),
        in_specs=[
            pl.BlockSpec(one, lambda at: (at, 0, 0, 0)),
            pl.BlockSpec(one, lambda at: (jnp.minimum(at, 1), 0, 0, 0)),
            pl.BlockSpec(one, lambda at: (jnp.maximum(at - 2, 0), 0, 0, 0)),
        ]
        + [ANYWHERE] * (1 + len(after)),
        out_specs=pl.BlockSpec(
            one, lambda at: (jnp.where(at < 2, at, MEMBERS - 4 + at), 0, 0, 0)
        ),
        input_output_aliases={3: 0},
        compiler_params=pltpu.CompilerParams(vmem_limit_bytes=16 << 20),
        cost_estimate=cost(3),
        name="whole_settle",
    )(near, below, above, summed, *after)


def gather_split_kernel(place, *refs):
    pieces, outs, sem = refs[:GROUP], refs[GROUP:-1], refs[-1]
    here = place[0] & (GROUP - 1)
    copies = []
    for away, piece in enumerate(pieces):
        start = (SHARE * (here ^ away) + CORES) * HEAD_DIM
        columns = pl.ds(pl.multiple_of(start, HEAD_DIM), HEAD_DIM)
        for index, out in enumerate(outs):
            copies.append((piece.at[index], out.at[:, columns]))
    copy_all(copies, sem)


def gather_split(place, pieces):
    return pl.pallas_call(
        gather_split_kernel,
        out_shape=[jax.ShapeDtypeStruct((BLOCK, HEADS * HEAD_DIM), jnp.bfloat16)] * 3,
        in_specs=[SCALARS] + [FAST] * GROUP,
        out_specs=[ANYWHERE] * 3,
        scratch_shapes=[pltpu.SemaphoreType.DMA((3 * GROUP,))],
        compiler_params=pltpu.CompilerParams(vmem_limit_bytes=16 << 20),
        cost_estimate=cost(3),
        name="gather_split",
    )(place, *pieces)


def gather_kernel(columns, count, *refs):
    outs, sem = refs[-1 - count : -1], refs[-1]
    copies = []
    for at, head in enumerate(columns):
        for index in range(count):
            copies.append((refs[0].at[at, index], outs[index].at[:, head_columns(head)]))
    copy_all(copies, sem)


def gather(columns, pieces, so_far=()):
    count, kept = pieces.shape[1], len(so_far)
    return pl.pallas_call(
        functools.partial(gather_kernel, columns, count),
        out_shape=[jax.ShapeDtypeStruct((BLOCK, HEADS * HEAD_DIM), jnp.bfloat16)] * count,
        in_specs=[FAST] + [ANYWHERE] * kept,
        out_specs=[ANYWHERE] * count,
        scratch_shapes=[pltpu.SemaphoreType.DMA((count * len(columns),))],
        input_output_aliases={1 + at: at for at in range(kept)},
        compiler_params=pltpu.CompilerParams(vmem_limit_bytes=8 << 20),
        cost_estimate=cost(3),
        name="gather",
    )(pieces, *so_far)


def shards(query_rows, key_rows, value_rows, out_grad, key_blocks, block_counts):
    chips = lax.axis_size("seq")
    chip = lax.axis_index("seq")
    core = lax.axis_index("head")
    place = jnp.stack([chip, core]).astype(jnp.int32)
    lists = key_blocks.reshape(-1)
    wide = [list(range(d, d + MEMBERS)) for d in range(0, CORES * chips, MEMBERS)]
    whole_heads = [SHARE * spot + at for spot in range(GROUP) for at in range(CORES)]

    def across(members):
        return [members[0]] + [
            lax.ppermute(members[away], "seq", [(c, c ^ away) for c in range(chips)])
            for away in range(1, GROUP)
        ]

    def regroup_wide(member):
        return lax.all_to_all(
            member, ("seq", "head"), split_axis=0, concat_axis=0, axis_index_groups=wide, tiled=True
        )

    def swap(member):
        return lax.ppermute(member, "head", [(0, 1), (1, 0)])

    def upward(member):
        return lax.ppermute(member, "seq", [(c, c + GROUP) for c in range(chips - GROUP)])

    def downward(member):
        return lax.ppermute(member, "seq", [(c + GROUP, c) for c in range(chips - GROUP)])

    def crosswise(member):
        pairs = [(2 * c + 1, 2 * (c + GROUP)) for c in range(chips - GROUP)]
        return lax.ppermute(member, ("seq", "head"), pairs + [(b, a) for a, b in pairs])

    sources = (key_rows, value_rows, query_rows, out_grad)
    split = across(pack_split(place, sources))
    keys, rows = pack(sources, whole_heads)
    keys = regroup_wide(keys)
    rows = regroup_wide(rows)
    ordered, low, high, cross = arrange(place, split, [])
    edges = [upward(high), downward(low), crosswise(cross)]
    queries, near, far, low, high, cross = split_grads(
        place, lists, block_counts, ordered, swap(ordered), edges, split, []
    )
    edges, far = [upward(high), downward(low), crosswise(cross)], swap(far)
    low, high = cut(
        place,
        keys,
        [lambda core: (0, 2, 2), lambda core: (MEMBERS - 2, 2, 2)],
        [],
    )
    whole_edges = [upward(high), downward(low)]
    split_done = split_settle(place, near, far, edges, queries, [])
    split_out = across(split_done)
    whole_queries, whole_sums, whole_near, low, high = whole_grads(
        place, lists, block_counts, keys, whole_edges, rows, []
    )
    below, above = upward(high), downward(low)
    whole_queries = regroup_wide(whole_queries)
    whole_sums = whole_settle(whole_near, below, above, whole_sums, [whole_queries])
    whole_out = regroup_wide(whole_sums)
    key_grad, value_grad, query_grad = gather_split(place, split_out)
    (query_grad,) = gather(whole_heads, whole_queries[:, None], (query_grad,))
    key_grad, value_grad = gather(whole_heads, whole_out, (key_grad, value_grad))
    return query_grad, key_grad, value_grad


def solution(mesh):
    rows = P(("seq", "head"), None)
    return jax.shard_map(
        shards,
        mesh=mesh,
        in_specs=(rows, rows, rows, rows, P(), P()),
        out_specs=(rows, rows, rows),
        check_vma=False,
    )
```

```python
import functools
import math

import jax
import jax.numpy as jnp
from jax import lax
from jax.experimental import pallas as pl
from jax.experimental.pallas import tpu as pltpu
from jax.sharding import PartitionSpec as P

HEADS = 12
HEAD_DIM = 128
BLOCK = 512
MAXK = 3
GROUP = 4
SHARE = HEADS // GROUP
OWN = GROUP + 2
SEEN = OWN + GROUP + 1
CORES = 2
MEMBERS = GROUP * CORES
SCALE = HEAD_DIM ** -0.5
LOG_SCALE = SCALE * math.log2(math.e)
COST_FLOPS, COST_BYTES = 3.45e+09, 9.00e+06
VMEM_LIMIT = 60 * 1024 * 1024

ANYWHERE = pl.BlockSpec(memory_space=pl.ANY)
SCALARS = pl.BlockSpec(memory_space=pltpu.SMEM)
FAST = pl.BlockSpec(memory_space=pltpu.VMEM)


def pair_rows(left, right):
    return lax.dot_general(
        left, right, (((1,), (1,)), ((), ())), preferred_element_type=jnp.float32
    )


def product(left, right):
    return jnp.dot(left, right, preferred_element_type=jnp.float32)


def copy_all(copies, sem):
    started = [
        pltpu.make_async_copy(source, target, sem.at[at])
        for at, (source, target) in enumerate(copies)
    ]
    for copy in started:
        copy.start()
    for copy in started:
        copy.wait()


def head_columns(head):
    return pl.ds(head * HEAD_DIM, HEAD_DIM)


def cost(microseconds):
    return pl.CostEstimate(
        flops=int(microseconds * COST_FLOPS),
        bytes_accessed=int(microseconds * COST_BYTES),
        transcendentals=0,
    )


def pack_split_kernel(place, key_rows, value_rows, query_rows, out_grad, *refs):
    outs, sem = refs[:-1], refs[-1]
    here = place[0] & (GROUP - 1)
    copies = []
    for away, out in enumerate(outs):
        start = (SHARE * (here ^ away) + CORES) * HEAD_DIM
        columns = pl.ds(pl.multiple_of(start, HEAD_DIM), HEAD_DIM)
        for index, source in enumerate((key_rows, value_rows, query_rows, out_grad)):
            copies.append((source.at[:, columns], out.at[index]))
    copy_all(copies, sem)


def pack_split(place, sources):
    out = jax.ShapeDtypeStruct((len(sources), BLOCK, HEAD_DIM), jnp.bfloat16)
    return pl.pallas_call(
        pack_split_kernel,
        out_shape=[out] * GROUP,
        in_specs=[SCALARS] + [ANYWHERE] * len(sources),
        out_specs=[FAST] * GROUP,
        scratch_shapes=[pltpu.SemaphoreType.DMA((GROUP * len(sources),))],
        compiler_params=pltpu.CompilerParams(vmem_limit_bytes=VMEM_LIMIT),
        cost_estimate=cost(4),
        name="pack_split",
    )(place, *sources)


def pack_kernel(heads, *refs):
    sources, outs, sem = refs[:4], refs[4:6], refs[6]
    copies = []
    for at, head in enumerate(heads):
        for index, source in enumerate(sources):
            target = outs[index // 2].at[at, index % 2]
            copies.append((source.at[:, pl.ds(head * HEAD_DIM, HEAD_DIM)], target))
    copy_all(copies, sem)


def pack(sources, heads):
    out = jax.ShapeDtypeStruct((len(heads), 2, BLOCK, HEAD_DIM), jnp.bfloat16)
    return pl.pallas_call(
        functools.partial(pack_kernel, heads),
        out_shape=[out] * 2,
        in_specs=[ANYWHERE] * 4,
        out_specs=[FAST] * 2,
        scratch_shapes=[pltpu.SemaphoreType.DMA((4 * len(heads),))],
        compiler_params=pltpu.CompilerParams(vmem_limit_bytes=VMEM_LIMIT),
        cost_estimate=cost(6),
        name="pack",
    )(*sources)


def arrange_kernel(waited, place, *refs):
    members = refs[:GROUP]
    ordered, low, high, cross, sem = refs[GROUP + waited :]
    here, core = place[0] & (GROUP - 1), place[1]
    pair = pl.ds(0, 2)
    copies = []
    for away, member in enumerate(members):
        copies.append(pltpu.make_async_copy(member.at[pair], ordered.at[here ^ away], sem.at[away]))
    for copy in copies:
        copy.start()
    for copy in copies:
        copy.wait()
    low[0] = ordered[0]
    high[0] = ordered[GROUP - 1]
    cross[0] = ordered[core * (GROUP - 1)]


def arrange(place, members, after=()):
    block = (2, BLOCK, HEAD_DIM)
    edge = jax.ShapeDtypeStruct((1,) + block, jnp.bfloat16)
    return pl.pallas_call(
        functools.partial(arrange_kernel, len(after)),
        out_shape=[jax.ShapeDtypeStruct((GROUP,) + block, jnp.bfloat16), edge, edge, edge],
        in_specs=[SCALARS] + [ANYWHERE] * (GROUP + len(after)),
        out_specs=[FAST] * 4,
        scratch_shapes=[pltpu.SemaphoreType.DMA((GROUP,))],
        compiler_params=pltpu.CompilerParams(vmem_limit_bytes=16 << 20),
        cost_estimate=cost(2.5),
        name="arrange",
    )(place, *members, *after)


def cut_kernel(pieces, place, member, *refs):
    outs, sem = refs[-1 - len(pieces) : -1], refs[-1]
    copies = []
    for piece, out in zip(pieces, outs):
        start, rows, parts = piece(place[1])
        copies.append((member.at[pl.ds(start, rows), pl.ds(0, parts)], out))
    copy_all(copies, sem)


def cut(place, member, pieces, after=()):
    shapes = [piece(0)[1:] + member.shape[2:] for piece in pieces]
    return pl.pallas_call(
        functools.partial(cut_kernel, pieces),
        out_shape=[jax.ShapeDtypeStruct(shape, member.dtype) for shape in shapes],
        in_specs=[SCALARS] + [ANYWHERE] * (1 + len(after)),
        out_specs=[FAST] * len(pieces),
        scratch_shapes=[pltpu.SemaphoreType.DMA((len(pieces),))],
        compiler_params=pltpu.CompilerParams(vmem_limit_bytes=16 << 20),
        cost_estimate=cost(1.5),
        name="cut",
    )(place, member, *after)


def grads_core(first, place_of, spots, block_of, keys, rows, sums, queries, lists, counts):
    def query_step(spot, carry):
        block = block_of(spot)
        count = counts[block]

        def live(slots):
            query_block, grad_block = rows[spot, 0], rows[spot, 1]
            places = [place_of(lists[block * MAXK + slot] - first) for slot in range(slots)]
            scores = [pair_rows(keys[at, 0], query_block) for at in places]
            peak = functools.reduce(
                jnp.maximum, [jnp.max(member, axis=0, keepdims=True) for member in scores]
            )
            grown = [jnp.exp2(member * LOG_SCALE - peak * LOG_SCALE) for member in scores]
            weight_grads = [pair_rows(keys[at, 1], grad_block) for at in places]
            total = sum(jnp.sum(member, axis=0, keepdims=True) for member in grown)
            share = 1.0 / total
            delta = share * sum(
                jnp.sum(member * other, axis=0, keepdims=True)
                for member, other in zip(grown, weight_grads)
            )
            query_sum = None
            for at, member, other in zip(places, grown, weight_grads):
                weights = member * share
                score_low = (weights * (other - delta)).astype(jnp.bfloat16)
                sums[at, 1] += product(weights.astype(jnp.bfloat16), grad_block)
                sums[at, 0] += product(score_low, query_block) * SCALE
                term = product(keys[at, 0].T, score_low)
                query_sum = term if query_sum is None else query_sum + term
            queries[spot] = (query_sum * SCALE).T.astype(jnp.bfloat16)

        for slots in range(1, MAXK + 1):
            pl.when(count == slots)(functools.partial(live, slots))
        return carry

    lax.fori_loop(0, spots, query_step, 0)


def begin(copies, sem):
    started = [
        pltpu.make_async_copy(source, target, sem.at[at])
        for at, (source, target) in enumerate(copies)
    ]
    for copy in started:
        copy.start()
    return started


def split_grads_kernel(waited, place, lists, counts, *refs):
    member, swapped, below, above, cross = refs[:5]
    rows_in = refs[5 : 5 + GROUP]
    refs = refs[5 + GROUP + waited :]
    query_out, near_out, far_out, low_out, high_out, cross_out = refs[:6]
    keys, rows, sums, queries, rounded, sem = refs[6:]
    chip, core = place[0], place[1]
    first = 2 * (chip & ~(GROUP - 1)) - 2
    here = chip & (GROUP - 1)
    copies = begin(
        [(part.at[pl.ds(2, 2)], rows.at[here ^ away]) for away, part in enumerate(rows_in)]
        + [
            (member, keys.at[pl.ds(1, GROUP)]),
            (swapped, keys.at[pl.ds(OWN, GROUP)]),
            (below.at[0], keys.at[0]),
            (above.at[0], keys.at[OWN - 1]),
            (cross.at[0], keys.at[SEEN - 1]),
        ],
        sem,
    )
    sums[...] = jnp.zeros_like(sums)
    for copy in copies:
        copy.wait()

    def place_of(offset):
        half = offset >> 1
        other = jnp.where((half >= 1) & (half <= GROUP), OWN - 1 + half, SEEN - 1)
        return jnp.where((offset & 1) == core, half, other)

    def block_of(spot):
        return first + 2 + 2 * spot + core

    grads_core(first, place_of, GROUP, block_of, keys, rows, sums, queries, lists, counts)
    copies = begin([(queries, query_out), (sums.at[pl.ds(1, GROUP)], near_out)], sem)
    for index, spot in enumerate((*range(OWN, OWN + GROUP), 0, OWN - 1, SEEN - 1)):
        rounded[index] = sums[spot].astype(jnp.bfloat16)
    more = begin(
        [
            (rounded.at[pl.ds(0, GROUP)], far_out),
            (rounded.at[pl.ds(GROUP, 1)], low_out),
            (rounded.at[pl.ds(GROUP + 1, 1)], high_out),
            (rounded.at[pl.ds(GROUP + 2, 1)], cross_out),
        ],
        sem.at[pl.ds(2, 4)],
    )
    for copy in copies + more:
        copy.wait()


def split_grads(place, lists, counts, member, swapped, edges, rows, after=()):
    block = (BLOCK, HEAD_DIM)
    edge = jax.ShapeDtypeStruct((1, 2) + block, jnp.bfloat16)
    outs = [
        jax.ShapeDtypeStruct((GROUP,) + block, jnp.bfloat16),
        jax.ShapeDtypeStruct((GROUP, 2) + block, jnp.float32),
        jax.ShapeDtypeStruct((GROUP, 2) + block, jnp.bfloat16),
        edge,
        edge,
        edge,
    ]
    return pl.pallas_call(
        functools.partial(split_grads_kernel, len(after)),
        out_shape=outs,
        in_specs=[SCALARS] * 3 + [ANYWHERE] * (5 + GROUP + len(after)),
        out_specs=[ANYWHERE] * len(outs),
        scratch_shapes=[
            pltpu.VMEM((SEEN, 2) + block, jnp.bfloat16),
            pltpu.VMEM((GROUP, 2) + block, jnp.bfloat16),
            pltpu.VMEM((SEEN, 2) + block, jnp.float32),
            pltpu.VMEM((GROUP,) + block, jnp.bfloat16),
            pltpu.VMEM((GROUP + 3, 2) + block, jnp.bfloat16),
            pltpu.SemaphoreType.DMA((GROUP + 5,)),
        ],
        compiler_params=pltpu.CompilerParams(vmem_limit_bytes=VMEM_LIMIT),
        cost_estimate=cost(13),
        name="split_grads",
    )(place, lists, counts, member, swapped, *edges, *rows, *after)


def whole_grads_kernel(waited, place, lists, counts, *refs):
    member, below, above, rows_in = refs[:4]
    refs = refs[4 + waited :]
    query_out, sum_out, edge_out, low_out, high_out = refs[:5]
    keys, rows, sums, queries, rounded, sem = refs[5:]
    first = 2 * (place[0] & ~(GROUP - 1)) - 2
    copies = begin(
        [
            (member, keys.at[pl.ds(2, MEMBERS)]),
            (below, keys.at[pl.ds(0, 2)]),
            (above, keys.at[pl.ds(MEMBERS + 2, 2)]),
            (rows_in, rows),
        ],
        sem,
    )
    sums[...] = jnp.zeros_like(sums)
    for copy in copies:
        copy.wait()
    grads_core(
        first, lambda offset: offset, MEMBERS, lambda spot: first + 2 + spot,
        keys, rows, sums, queries, lists, counts,
    )
    copies = begin(
        [
            (queries, query_out),
            (sums.at[pl.ds(2, 2)], edge_out.at[pl.ds(0, 2)]),
            (sums.at[pl.ds(MEMBERS, 2)], edge_out.at[pl.ds(2, 2)]),
        ],
        sem,
    )
    rounded[...] = sums[...].astype(jnp.bfloat16)
    more = begin(
        [
            (rounded.at[pl.ds(2, MEMBERS)], sum_out),
            (rounded.at[pl.ds(0, 2)], low_out),
            (rounded.at[pl.ds(MEMBERS + 2, 2)], high_out),
        ],
        sem.at[pl.ds(3, 3)],
    )
    for copy in copies + more:
        copy.wait()


def whole_grads(place, lists, counts, member, edges, rows, after=()):
    block = (BLOCK, HEAD_DIM)
    edge = jax.ShapeDtypeStruct((2, 2) + block, jnp.bfloat16)
    outs = [
        jax.ShapeDtypeStruct((MEMBERS,) + block, jnp.bfloat16),
        jax.ShapeDtypeStruct((MEMBERS, 2) + block, jnp.bfloat16),
        jax.ShapeDtypeStruct((4, 2) + block, jnp.float32),
        edge,
        edge,
    ]
    return pl.pallas_call(
        functools.partial(whole_grads_kernel, len(after)),
        out_shape=outs,
        in_specs=[SCALARS] * 3 + [ANYWHERE] * (4 + len(after)),
        out_specs=[ANYWHERE] * len(outs),
        scratch_shapes=[
            pltpu.VMEM((MEMBERS + 4, 2) + block, jnp.bfloat16),
            pltpu.VMEM((MEMBERS, 2) + block, jnp.bfloat16),
            pltpu.VMEM((MEMBERS + 4, 2) + block, jnp.float32),
            pltpu.VMEM((MEMBERS,) + block, jnp.bfloat16),
            pltpu.VMEM((MEMBERS + 4, 2) + block, jnp.bfloat16),
            pltpu.SemaphoreType.DMA((6,)),
        ],
        compiler_params=pltpu.CompilerParams(vmem_limit_bytes=VMEM_LIMIT),
        cost_estimate=cost(22),
        name="whole_grads",
    )(place, lists, counts, member, *edges, rows, *after)


def split_settle_kernel(waited, place, near, far, below, above, cross, queries, *refs):
    outs = refs[waited:]
    here, core = place[0] & (GROUP - 1), place[1]
    for away, out in enumerate(outs):
        spot = here ^ away
        out[:2] = (near[spot] + far[spot].astype(jnp.float32)).astype(jnp.bfloat16)
        out[2] = queries[spot]

        def more(out, spot, *edges):
            total = near[spot] + far[spot].astype(jnp.float32)
            for edge in edges:
                total += edge[0].astype(jnp.float32)
            out[:2] = total.astype(jnp.bfloat16)

        low, high = spot == 0, spot == GROUP - 1
        pl.when(low & (core == 0))(functools.partial(more, out, spot, below, cross))
        pl.when(low & (core == 1))(functools.partial(more, out, spot, below))
        pl.when(high & (core == 0))(functools.partial(more, out, spot, above))
        pl.when(high & (core == 1))(functools.partial(more, out, spot, above, cross))


def split_settle(place, near, far, edges, queries, after=()):
    out = jax.ShapeDtypeStruct((3, BLOCK, HEAD_DIM), jnp.bfloat16)
    return pl.pallas_call(
        functools.partial(split_settle_kernel, len(after)),
        out_shape=[out] * GROUP,
        in_specs=[SCALARS] + [FAST] * 6 + [ANYWHERE] * len(after),
        out_specs=[FAST] * GROUP,
        compiler_params=pltpu.CompilerParams(vmem_limit_bytes=VMEM_LIMIT),
        cost_estimate=cost(4),
        name="split_settle",
    )(place, near, far, *edges, queries, *after)


def whole_settle_kernel(near, below, above, summed, *refs):
    out = refs[-1]
    at = pl.program_id(0)

    @pl.when(at < 2)
    def _():
        out[...] = (near[...] + below[...].astype(jnp.float32)).astype(jnp.bfloat16)

    @pl.when(at >= 2)
    def _():
        out[...] = (near[...] + above[...].astype(jnp.float32)).astype(jnp.bfloat16)


def whole_settle(near, below, above, summed, after=()):
    one = (1, 2, BLOCK, HEAD_DIM)
    return pl.pallas_call(
        whole_settle_kernel,
        grid=(4,),
        out_shape=jax.ShapeDtypeStruct(summed.shape, summed.dtype),
        in_specs=[
            pl.BlockSpec(one, lambda at: (at, 0, 0, 0)),
            pl.BlockSpec(one, lambda at: (jnp.minimum(at, 1), 0, 0, 0)),
            pl.BlockSpec(one, lambda at: (jnp.maximum(at - 2, 0), 0, 0, 0)),
        ]
        + [ANYWHERE] * (1 + len(after)),
        out_specs=pl.BlockSpec(
            one, lambda at: (jnp.where(at < 2, at, MEMBERS - 4 + at), 0, 0, 0)
        ),
        input_output_aliases={3: 0},
        compiler_params=pltpu.CompilerParams(vmem_limit_bytes=16 << 20),
        cost_estimate=cost(3),
        name="whole_settle",
    )(near, below, above, summed, *after)


def gather_split_kernel(place, *refs):
    pieces, outs, sem = refs[:GROUP], refs[GROUP:-1], refs[-1]
    here = place[0] & (GROUP - 1)
    copies = []
    for away, piece in enumerate(pieces):
        start = (SHARE * (here ^ away) + CORES) * HEAD_DIM
        columns = pl.ds(pl.multiple_of(start, HEAD_DIM), HEAD_DIM)
        for index, out in enumerate(outs):
            copies.append((piece.at[index], out.at[:, columns]))
    copy_all(copies, sem)


def gather_split(place, pieces):
    return pl.pallas_call(
        gather_split_kernel,
        out_shape=[jax.ShapeDtypeStruct((BLOCK, HEADS * HEAD_DIM), jnp.bfloat16)] * 3,
        in_specs=[SCALARS] + [FAST] * GROUP,
        out_specs=[ANYWHERE] * 3,
        scratch_shapes=[pltpu.SemaphoreType.DMA((3 * GROUP,))],
        compiler_params=pltpu.CompilerParams(vmem_limit_bytes=16 << 20),
        cost_estimate=cost(3),
        name="gather_split",
    )(place, *pieces)


def gather_kernel(columns, count, *refs):
    outs, sem = refs[-1 - count : -1], refs[-1]
    copies = []
    for at, head in enumerate(columns):
        for index in range(count):
            copies.append((refs[0].at[at, index], outs[index].at[:, head_columns(head)]))
    copy_all(copies, sem)


def gather(columns, pieces, so_far=()):
    count, kept = pieces.shape[1], len(so_far)
    return pl.pallas_call(
        functools.partial(gather_kernel, columns, count),
        out_shape=[jax.ShapeDtypeStruct((BLOCK, HEADS * HEAD_DIM), jnp.bfloat16)] * count,
        in_specs=[FAST] + [ANYWHERE] * kept,
        out_specs=[ANYWHERE] * count,
        scratch_shapes=[pltpu.SemaphoreType.DMA((count * len(columns),))],
        input_output_aliases={1 + at: at for at in range(kept)},
        compiler_params=pltpu.CompilerParams(vmem_limit_bytes=8 << 20),
        cost_estimate=cost(3),
        name="gather",
    )(pieces, *so_far)


def shards(query_rows, key_rows, value_rows, out_grad, key_blocks, block_counts):
    chips = lax.axis_size("seq")
    chip = lax.axis_index("seq")
    core = lax.axis_index("head")
    place = jnp.stack([chip, core]).astype(jnp.int32)
    lists = key_blocks.reshape(-1)
    wide = [list(range(d, d + MEMBERS)) for d in range(0, CORES * chips, MEMBERS)]
    whole_heads = [SHARE * spot + at for spot in range(GROUP) for at in range(CORES)]

    def across(members):
        return [members[0]] + [
            lax.ppermute(members[away], "seq", [(c, c ^ away) for c in range(chips)])
            for away in range(1, GROUP)
        ]

    def regroup_wide(member):
        return lax.all_to_all(
            member, ("seq", "head"), split_axis=0, concat_axis=0, axis_index_groups=wide, tiled=True
        )

    def swap(member):
        return lax.ppermute(member, "head", [(0, 1), (1, 0)])

    def upward(member):
        return lax.ppermute(member, "seq", [(c, c + GROUP) for c in range(chips - GROUP)])

    def downward(member):
        return lax.ppermute(member, "seq", [(c + GROUP, c) for c in range(chips - GROUP)])

    def crosswise(member):
        pairs = [(2 * c + 1, 2 * (c + GROUP)) for c in range(chips - GROUP)]
        return lax.ppermute(member, ("seq", "head"), pairs + [(b, a) for a, b in pairs])

    sources = (key_rows, value_rows, query_rows, out_grad)
    split = across(pack_split(place, sources))
    keys, rows = pack(sources, whole_heads)
    keys = regroup_wide(keys)
    rows = regroup_wide(rows)
    ordered, low, high, cross = arrange(place, split, [])
    edges = [upward(high), downward(low), crosswise(cross)]
    queries, near, far, low, high, cross = split_grads(
        place, lists, block_counts, ordered, swap(ordered), edges, split, []
    )
    edges, far = [upward(high), downward(low), crosswise(cross)], swap(far)
    low, high = cut(
        place,
        keys,
        [lambda core: (0, 2, 2), lambda core: (MEMBERS - 2, 2, 2)],
        [],
    )
    whole_edges = [upward(high), downward(low)]
    split_done = split_settle(place, near, far, edges, queries, [])
    split_out = across(split_done)
    whole_queries, whole_sums, whole_near, low, high = whole_grads(
        place, lists, block_counts, keys, whole_edges, rows, []
    )
    below, above = upward(high), downward(low)
    whole_queries = regroup_wide(whole_queries)
    whole_sums = whole_settle(whole_near, below, above, whole_sums, [whole_queries])
    whole_out = regroup_wide(whole_sums)
    key_grad, value_grad, query_grad = gather_split(place, split_out)
    (query_grad,) = gather(whole_heads, whole_queries[:, None], (query_grad,))
    key_grad, value_grad = gather(whole_heads, whole_out, (key_grad, value_grad))
    return query_grad, key_grad, value_grad


def solution(mesh):
    rows = P(("seq", "head"), None)
    return jax.shard_map(
        shards,
        mesh=mesh,
        in_specs=(rows, rows, rows, rows, P(), P()),
        out_specs=(rows, rows, rows),
        check_vma=False,
    )
```

```python
import functools
import math

import jax
import jax.numpy as jnp
from jax import lax
from jax.experimental import pallas as pl
from jax.experimental.pallas import tpu as pltpu
from jax.sharding import PartitionSpec as P

HEADS = 12
HEAD_DIM = 128
BLOCK = 512
MAXK = 3
GROUP = 4
SHARE = HEADS // GROUP
OWN = GROUP + 2
SEEN = OWN + GROUP + 1
CORES = 2
MEMBERS = GROUP * CORES
SCALE = HEAD_DIM ** -0.5
LOG_SCALE = SCALE * math.log2(math.e)
COST_FLOPS, COST_BYTES = 4.02e+09, 1.05e+07
VMEM_LIMIT = 60 * 1024 * 1024

ANYWHERE = pl.BlockSpec(memory_space=pl.ANY)
SCALARS = pl.BlockSpec(memory_space=pltpu.SMEM)
FAST = pl.BlockSpec(memory_space=pltpu.VMEM)


def pair_rows(left, right):
    return lax.dot_general(
        left, right, (((1,), (1,)), ((), ())), preferred_element_type=jnp.float32
    )


def product(left, right):
    return jnp.dot(left, right, preferred_element_type=jnp.float32)


def copy_all(copies, sem):
    started = [
        pltpu.make_async_copy(source, target, sem.at[at])
        for at, (source, target) in enumerate(copies)
    ]
    for copy in started:
        copy.start()
    for copy in started:
        copy.wait()


def head_columns(head):
    return pl.ds(head * HEAD_DIM, HEAD_DIM)


def cost(microseconds):
    return pl.CostEstimate(
        flops=int(microseconds * COST_FLOPS),
        bytes_accessed=int(microseconds * COST_BYTES),
        transcendentals=0,
    )


def pack_split_kernel(place, key_rows, value_rows, query_rows, out_grad, *refs):
    outs, sem = refs[:-1], refs[-1]
    here = place[0] & (GROUP - 1)
    copies = []
    for away, out in enumerate(outs):
        start = (SHARE * (here ^ away) + CORES) * HEAD_DIM
        columns = pl.ds(pl.multiple_of(start, HEAD_DIM), HEAD_DIM)
        for index, source in enumerate((key_rows, value_rows, query_rows, out_grad)):
            copies.append((source.at[:, columns], out.at[index]))
    copy_all(copies, sem)


def pack_split(place, sources):
    out = jax.ShapeDtypeStruct((len(sources), BLOCK, HEAD_DIM), jnp.bfloat16)
    return pl.pallas_call(
        pack_split_kernel,
        out_shape=[out] * GROUP,
        in_specs=[SCALARS] + [ANYWHERE] * len(sources),
        out_specs=[FAST] * GROUP,
        scratch_shapes=[pltpu.SemaphoreType.DMA((GROUP * len(sources),))],
        compiler_params=pltpu.CompilerParams(vmem_limit_bytes=VMEM_LIMIT),
        cost_estimate=cost(4),
        name="pack_split",
    )(place, *sources)


def pack_kernel(heads, *refs):
    sources, outs, sem = refs[:4], refs[4:6], refs[6]
    copies = []
    for at, head in enumerate(heads):
        for index, source in enumerate(sources):
            target = outs[index // 2].at[at, index % 2]
            copies.append((source.at[:, pl.ds(head * HEAD_DIM, HEAD_DIM)], target))
    copy_all(copies, sem)


def pack(sources, heads):
    out = jax.ShapeDtypeStruct((len(heads), 2, BLOCK, HEAD_DIM), jnp.bfloat16)
    return pl.pallas_call(
        functools.partial(pack_kernel, heads),
        out_shape=[out] * 2,
        in_specs=[ANYWHERE] * 4,
        out_specs=[FAST] * 2,
        scratch_shapes=[pltpu.SemaphoreType.DMA((4 * len(heads),))],
        compiler_params=pltpu.CompilerParams(vmem_limit_bytes=VMEM_LIMIT),
        cost_estimate=cost(6),
        name="pack",
    )(*sources)


def arrange_kernel(waited, place, *refs):
    members = refs[:GROUP]
    ordered, low, high, cross, sem = refs[GROUP + waited :]
    here, core = place[0] & (GROUP - 1), place[1]
    pair = pl.ds(0, 2)
    copies = []
    for away, member in enumerate(members):
        copies.append(pltpu.make_async_copy(member.at[pair], ordered.at[here ^ away], sem.at[away]))
    for copy in copies:
        copy.start()
    for copy in copies:
        copy.wait()
    low[0] = ordered[0]
    high[0] = ordered[GROUP - 1]
    cross[0] = ordered[core * (GROUP - 1)]


def arrange(place, members, after=()):
    block = (2, BLOCK, HEAD_DIM)
    edge = jax.ShapeDtypeStruct((1,) + block, jnp.bfloat16)
    return pl.pallas_call(
        functools.partial(arrange_kernel, len(after)),
        out_shape=[jax.ShapeDtypeStruct((GROUP,) + block, jnp.bfloat16), edge, edge, edge],
        in_specs=[SCALARS] + [ANYWHERE] * (GROUP + len(after)),
        out_specs=[FAST] * 4,
        scratch_shapes=[pltpu.SemaphoreType.DMA((GROUP,))],
        compiler_params=pltpu.CompilerParams(vmem_limit_bytes=16 << 20),
        cost_estimate=cost(2.5),
        name="arrange",
    )(place, *members, *after)


def cut_kernel(pieces, place, member, *refs):
    outs, sem = refs[-1 - len(pieces) : -1], refs[-1]
    copies = []
    for piece, out in zip(pieces, outs):
        start, rows, parts = piece(place[1])
        copies.append((member.at[pl.ds(start, rows), pl.ds(0, parts)], out))
    copy_all(copies, sem)


def cut(place, member, pieces, after=()):
    shapes = [piece(0)[1:] + member.shape[2:] for piece in pieces]
    return pl.pallas_call(
        functools.partial(cut_kernel, pieces),
        out_shape=[jax.ShapeDtypeStruct(shape, member.dtype) for shape in shapes],
        in_specs=[SCALARS] + [ANYWHERE] * (1 + len(after)),
        out_specs=[FAST] * len(pieces),
        scratch_shapes=[pltpu.SemaphoreType.DMA((len(pieces),))],
        compiler_params=pltpu.CompilerParams(vmem_limit_bytes=16 << 20),
        cost_estimate=cost(1.5),
        name="cut",
    )(place, member, *after)


def grads_core(
    first, place_of, spots, block_of, keys, rows, sums, queries, lists, counts, after_spot=None
):
    def query_step(spot, carry):
        block = block_of(spot)
        count = counts[block]

        def live(slots):
            query_block, grad_block = rows[spot, 0], rows[spot, 1]
            places = [place_of(lists[block * MAXK + slot] - first) for slot in range(slots)]
            scores = [pair_rows(keys[at, 0], query_block) for at in places]
            peak = functools.reduce(
                jnp.maximum, [jnp.max(member, axis=0, keepdims=True) for member in scores]
            )
            grown = [jnp.exp2(member * LOG_SCALE - peak * LOG_SCALE) for member in scores]
            weight_grads = [pair_rows(keys[at, 1], grad_block) for at in places]
            total = sum(jnp.sum(member, axis=0, keepdims=True) for member in grown)
            share = 1.0 / total
            delta = share * sum(
                jnp.sum(member * other, axis=0, keepdims=True)
                for member, other in zip(grown, weight_grads)
            )
            query_sum = None
            for at, member, other in zip(places, grown, weight_grads):
                weights = member * share
                score_low = (weights * (other - delta)).astype(jnp.bfloat16)
                sums[at, 1] += product(weights.astype(jnp.bfloat16), grad_block)
                sums[at, 0] += product(score_low, query_block) * SCALE
                term = product(keys[at, 0].T, score_low)
                query_sum = term if query_sum is None else query_sum + term
            queries[spot] = (query_sum * SCALE).T.astype(jnp.bfloat16)

        for slots in range(1, MAXK + 1):
            pl.when(count == slots)(functools.partial(live, slots))
        if after_spot is not None:
            after_spot(spot)
        return carry

    lax.fori_loop(0, spots, query_step, 0)


def begin(copies, sem):
    started = [
        pltpu.make_async_copy(source, target, sem.at[at])
        for at, (source, target) in enumerate(copies)
    ]
    for copy in started:
        copy.start()
    return started


def split_grads_kernel(waited, place, lists, counts, *refs):
    member, swapped, below, above, cross = refs[:5]
    rows_in = refs[5 : 5 + GROUP]
    refs = refs[5 + GROUP + waited :]
    query_out, near_out, far_out, low_out, high_out, cross_out = refs[:6]
    keys, rows, sums, queries, rounded, sem = refs[6:]
    chip, core = place[0], place[1]
    first = 2 * (chip & ~(GROUP - 1)) - 2
    here = chip & (GROUP - 1)
    copies = begin(
        [(part.at[pl.ds(2, 2)], rows.at[here ^ away]) for away, part in enumerate(rows_in)]
        + [
            (member, keys.at[pl.ds(1, GROUP)]),
            (swapped, keys.at[pl.ds(OWN, GROUP)]),
            (below.at[0], keys.at[0]),
            (above.at[0], keys.at[OWN - 1]),
            (cross.at[0], keys.at[SEEN - 1]),
        ],
        sem,
    )
    sums[...] = jnp.zeros_like(sums)
    for copy in copies:
        copy.wait()

    def place_of(offset):
        half = offset >> 1
        other = jnp.where((half >= 1) & (half <= GROUP), OWN - 1 + half, SEEN - 1)
        return jnp.where((offset & 1) == core, half, other)

    def block_of(spot):
        return first + 2 + 2 * spot + core

    grads_core(first, place_of, GROUP, block_of, keys, rows, sums, queries, lists, counts)
    copies = begin([(queries, query_out), (sums.at[pl.ds(1, GROUP)], near_out)], sem)
    for index, spot in enumerate((*range(OWN, OWN + GROUP), 0, OWN - 1, SEEN - 1)):
        rounded[index] = sums[spot].astype(jnp.bfloat16)
    more = begin(
        [
            (rounded.at[pl.ds(0, GROUP)], far_out),
            (rounded.at[pl.ds(GROUP, 1)], low_out),
            (rounded.at[pl.ds(GROUP + 1, 1)], high_out),
            (rounded.at[pl.ds(GROUP + 2, 1)], cross_out),
        ],
        sem.at[pl.ds(2, 4)],
    )
    for copy in copies + more:
        copy.wait()


def split_grads(place, lists, counts, member, swapped, edges, rows, after=()):
    block = (BLOCK, HEAD_DIM)
    edge = jax.ShapeDtypeStruct((1, 2) + block, jnp.bfloat16)
    outs = [
        jax.ShapeDtypeStruct((GROUP,) + block, jnp.bfloat16),
        jax.ShapeDtypeStruct((GROUP, 2) + block, jnp.float32),
        jax.ShapeDtypeStruct((GROUP, 2) + block, jnp.bfloat16),
        edge,
        edge,
        edge,
    ]
    return pl.pallas_call(
        functools.partial(split_grads_kernel, len(after)),
        out_shape=outs,
        in_specs=[SCALARS] * 3 + [ANYWHERE] * (5 + GROUP + len(after)),
        out_specs=[ANYWHERE] * len(outs),
        scratch_shapes=[
            pltpu.VMEM((SEEN, 2) + block, jnp.bfloat16),
            pltpu.VMEM((GROUP, 2) + block, jnp.bfloat16),
            pltpu.VMEM((SEEN, 2) + block, jnp.float32),
            pltpu.VMEM((GROUP,) + block, jnp.bfloat16),
            pltpu.VMEM((GROUP + 3, 2) + block, jnp.bfloat16),
            pltpu.SemaphoreType.DMA((GROUP + 5,)),
        ],
        compiler_params=pltpu.CompilerParams(vmem_limit_bytes=VMEM_LIMIT),
        cost_estimate=cost(13),
        name="split_grads",
    )(place, lists, counts, member, swapped, *edges, *rows, *after)


def whole_grads_kernel(waited, place, lists, counts, *refs):
    member, below, above, rows_in = refs[:4]
    refs = refs[4 + waited :]
    query_out, sum_out, edge_out, low_out, high_out = refs[:5]
    keys, rows, sums, queries, rounded, sem = refs[5:]
    first = 2 * (place[0] & ~(GROUP - 1)) - 2
    copies = begin(
        [
            (member, keys.at[pl.ds(2, MEMBERS)]),
            (below, keys.at[pl.ds(0, 2)]),
            (above, keys.at[pl.ds(MEMBERS + 2, 2)]),
            (rows_in, rows),
        ],
        sem,
    )
    sums[...] = jnp.zeros_like(sums)
    for copy in copies:
        copy.wait()

    def query_copy(spot):
        return pltpu.make_async_copy(queries.at[spot], query_out.at[spot], sem.at[4 + spot])

    def low_copy(spot):
        return pltpu.make_async_copy(rounded.at[spot], low_out.at[spot], sem.at[12 + spot])

    def sum_copy(spot):
        return pltpu.make_async_copy(rounded.at[spot], sum_out.at[spot - 2], sem.at[12 + spot])

    def after_spot(spot):
        rounded[spot] = sums[spot].astype(jnp.bfloat16)
        query_copy(spot).start()
        pl.when(spot < 2)(lambda: low_copy(spot).start())
        pl.when(spot >= 2)(lambda: sum_copy(spot).start())

    grads_core(
        first, lambda offset: offset, MEMBERS, lambda spot: first + 2 + spot,
        keys, rows, sums, queries, lists, counts, after_spot,
    )
    copies = begin(
        [
            (sums.at[pl.ds(2, 2)], edge_out.at[pl.ds(0, 2)]),
            (sums.at[pl.ds(MEMBERS, 2)], edge_out.at[pl.ds(2, 2)]),
        ],
        sem,
    )
    rounded[MEMBERS:] = sums[MEMBERS:].astype(jnp.bfloat16)
    copies += begin(
        [
            (rounded.at[pl.ds(MEMBERS, 2)], sum_out.at[pl.ds(MEMBERS - 2, 2)]),
            (rounded.at[pl.ds(MEMBERS + 2, 2)], high_out),
        ],
        sem.at[pl.ds(2, 2)],
    )
    for spot in range(MEMBERS):
        copies.append(query_copy(spot))
        copies.append(low_copy(spot) if spot < 2 else sum_copy(spot))
    for copy in copies:
        copy.wait()


def whole_grads(place, lists, counts, member, edges, rows, after=()):
    block = (BLOCK, HEAD_DIM)
    edge = jax.ShapeDtypeStruct((2, 2) + block, jnp.bfloat16)
    outs = [
        jax.ShapeDtypeStruct((MEMBERS,) + block, jnp.bfloat16),
        jax.ShapeDtypeStruct((MEMBERS, 2) + block, jnp.bfloat16),
        jax.ShapeDtypeStruct((4, 2) + block, jnp.float32),
        edge,
        edge,
    ]
    return pl.pallas_call(
        functools.partial(whole_grads_kernel, len(after)),
        out_shape=outs,
        in_specs=[SCALARS] * 3 + [ANYWHERE] * (4 + len(after)),
        out_specs=[ANYWHERE] * len(outs),
        scratch_shapes=[
            pltpu.VMEM((MEMBERS + 4, 2) + block, jnp.bfloat16),
            pltpu.VMEM((MEMBERS, 2) + block, jnp.bfloat16),
            pltpu.VMEM((MEMBERS + 4, 2) + block, jnp.float32),
            pltpu.VMEM((MEMBERS,) + block, jnp.bfloat16),
            pltpu.VMEM((MEMBERS + 4, 2) + block, jnp.bfloat16),
            pltpu.SemaphoreType.DMA((2 * MEMBERS + 4,)),
        ],
        compiler_params=pltpu.CompilerParams(vmem_limit_bytes=VMEM_LIMIT),
        cost_estimate=cost(22),
        name="whole_grads",
    )(place, lists, counts, member, *edges, rows, *after)


def split_settle_kernel(waited, place, near, far, below, above, cross, queries, *refs):
    outs = refs[waited:]
    here, core = place[0] & (GROUP - 1), place[1]
    for away, out in enumerate(outs):
        spot = here ^ away
        out[:2] = (near[spot] + far[spot].astype(jnp.float32)).astype(jnp.bfloat16)
        out[2] = queries[spot]

        def more(out, spot, *edges):
            total = near[spot] + far[spot].astype(jnp.float32)
            for edge in edges:
                total += edge[0].astype(jnp.float32)
            out[:2] = total.astype(jnp.bfloat16)

        low, high = spot == 0, spot == GROUP - 1
        pl.when(low & (core == 0))(functools.partial(more, out, spot, below, cross))
        pl.when(low & (core == 1))(functools.partial(more, out, spot, below))
        pl.when(high & (core == 0))(functools.partial(more, out, spot, above))
        pl.when(high & (core == 1))(functools.partial(more, out, spot, above, cross))


def split_settle(place, near, far, edges, queries, after=()):
    out = jax.ShapeDtypeStruct((3, BLOCK, HEAD_DIM), jnp.bfloat16)
    return pl.pallas_call(
        functools.partial(split_settle_kernel, len(after)),
        out_shape=[out] * GROUP,
        in_specs=[SCALARS] + [FAST] * 6 + [ANYWHERE] * len(after),
        out_specs=[FAST] * GROUP,
        compiler_params=pltpu.CompilerParams(vmem_limit_bytes=VMEM_LIMIT),
        cost_estimate=cost(4),
        name="split_settle",
    )(place, near, far, *edges, queries, *after)


def whole_settle_kernel(near, below, above, summed, *refs):
    out = refs[-1]
    at = pl.program_id(0)

    @pl.when(at < 2)
    def _():
        out[...] = (near[...] + below[...].astype(jnp.float32)).astype(jnp.bfloat16)

    @pl.when(at >= 2)
    def _():
        out[...] = (near[...] + above[...].astype(jnp.float32)).astype(jnp.bfloat16)


def whole_settle(near, below, above, summed, after=()):
    one = (1, 2, BLOCK, HEAD_DIM)
    return pl.pallas_call(
        whole_settle_kernel,
        grid=(4,),
        out_shape=jax.ShapeDtypeStruct(summed.shape, summed.dtype),
        in_specs=[
            pl.BlockSpec(one, lambda at: (at, 0, 0, 0)),
            pl.BlockSpec(one, lambda at: (jnp.minimum(at, 1), 0, 0, 0)),
            pl.BlockSpec(one, lambda at: (jnp.maximum(at - 2, 0), 0, 0, 0)),
        ]
        + [ANYWHERE] * (1 + len(after)),
        out_specs=pl.BlockSpec(
            one, lambda at: (jnp.where(at < 2, at, MEMBERS - 4 + at), 0, 0, 0)
        ),
        input_output_aliases={3: 0},
        compiler_params=pltpu.CompilerParams(vmem_limit_bytes=16 << 20),
        cost_estimate=cost(3),
        name="whole_settle",
    )(near, below, above, summed, *after)


def gather_split_kernel(place, *refs):
    pieces, outs, sem = refs[:GROUP], refs[GROUP:-1], refs[-1]
    here = place[0] & (GROUP - 1)
    copies = []
    for away, piece in enumerate(pieces):
        start = (SHARE * (here ^ away) + CORES) * HEAD_DIM
        columns = pl.ds(pl.multiple_of(start, HEAD_DIM), HEAD_DIM)
        for index, out in enumerate(outs):
            copies.append((piece.at[index], out.at[:, columns]))
    copy_all(copies, sem)


def gather_split(place, pieces):
    return pl.pallas_call(
        gather_split_kernel,
        out_shape=[jax.ShapeDtypeStruct((BLOCK, HEADS * HEAD_DIM), jnp.bfloat16)] * 3,
        in_specs=[SCALARS] + [FAST] * GROUP,
        out_specs=[ANYWHERE] * 3,
        scratch_shapes=[pltpu.SemaphoreType.DMA((3 * GROUP,))],
        compiler_params=pltpu.CompilerParams(vmem_limit_bytes=16 << 20),
        cost_estimate=cost(3),
        name="gather_split",
    )(place, *pieces)


def gather_kernel(columns, count, *refs):
    outs, sem = refs[-1 - count : -1], refs[-1]
    copies = []
    for at, head in enumerate(columns):
        for index in range(count):
            copies.append((refs[0].at[at, index], outs[index].at[:, head_columns(head)]))
    copy_all(copies, sem)


def gather(columns, pieces, so_far=()):
    count, kept = pieces.shape[1], len(so_far)
    return pl.pallas_call(
        functools.partial(gather_kernel, columns, count),
        out_shape=[jax.ShapeDtypeStruct((BLOCK, HEADS * HEAD_DIM), jnp.bfloat16)] * count,
        in_specs=[FAST] + [ANYWHERE] * kept,
        out_specs=[ANYWHERE] * count,
        scratch_shapes=[pltpu.SemaphoreType.DMA((count * len(columns),))],
        input_output_aliases={1 + at: at for at in range(kept)},
        compiler_params=pltpu.CompilerParams(vmem_limit_bytes=8 << 20),
        cost_estimate=cost(3),
        name="gather",
    )(pieces, *so_far)


def shards(query_rows, key_rows, value_rows, out_grad, key_blocks, block_counts):
    chips = lax.axis_size("seq")
    chip = lax.axis_index("seq")
    core = lax.axis_index("head")
    place = jnp.stack([chip, core]).astype(jnp.int32)
    lists = key_blocks.reshape(-1)
    wide = [list(range(d, d + MEMBERS)) for d in range(0, CORES * chips, MEMBERS)]
    whole_heads = [SHARE * spot + at for spot in range(GROUP) for at in range(CORES)]

    def across(members):
        return [members[0]] + [
            lax.ppermute(members[away], "seq", [(c, c ^ away) for c in range(chips)])
            for away in range(1, GROUP)
        ]

    def regroup_wide(member):
        return lax.all_to_all(
            member, ("seq", "head"), split_axis=0, concat_axis=0, axis_index_groups=wide, tiled=True
        )

    def swap(member):
        return lax.ppermute(member, "head", [(0, 1), (1, 0)])

    def upward(member):
        return lax.ppermute(member, "seq", [(c, c + GROUP) for c in range(chips - GROUP)])

    def downward(member):
        return lax.ppermute(member, "seq", [(c + GROUP, c) for c in range(chips - GROUP)])

    def crosswise(member):
        pairs = [(2 * c + 1, 2 * (c + GROUP)) for c in range(chips - GROUP)]
        return lax.ppermute(member, ("seq", "head"), pairs + [(b, a) for a, b in pairs])

    sources = (key_rows, value_rows, query_rows, out_grad)
    split = across(pack_split(place, sources))
    keys, rows = pack(sources, whole_heads)
    keys = regroup_wide(keys)
    rows = regroup_wide(rows)
    ordered, low, high, cross = arrange(place, split, [])
    edges = [upward(high), downward(low), crosswise(cross)]
    queries, near, far, low, high, cross = split_grads(
        place, lists, block_counts, ordered, swap(ordered), edges, split, []
    )
    edges, far = [upward(high), downward(low), crosswise(cross)], swap(far)
    low, high = cut(
        place,
        keys,
        [lambda core: (0, 2, 2), lambda core: (MEMBERS - 2, 2, 2)],
        [],
    )
    whole_edges = [upward(high), downward(low)]
    split_done = split_settle(place, near, far, edges, queries, [])
    split_out = across(split_done)
    whole_queries, whole_sums, whole_near, low, high = whole_grads(
        place, lists, block_counts, keys, whole_edges, rows, []
    )
    below, above = upward(high), downward(low)
    whole_queries = regroup_wide(whole_queries)
    whole_sums = whole_settle(whole_near, below, above, whole_sums, [whole_queries])
    whole_out = regroup_wide(whole_sums)
    key_grad, value_grad, query_grad = gather_split(place, split_out)
    (query_grad,) = gather(whole_heads, whole_queries[:, None], (query_grad,))
    key_grad, value_grad = gather(whole_heads, whole_out, (key_grad, value_grad))
    return query_grad, key_grad, value_grad


def solution(mesh):
    rows = P(("seq", "head"), None)
    return jax.shard_map(
        shards,
        mesh=mesh,
        in_specs=(rows, rows, rows, rows, P(), P()),
        out_specs=(rows, rows, rows),
        check_vma=False,
    )
```
